256 devices in a mesh: seq: 16 (over y, x_hi, core), ch: 16 (over z, x_lo).
Axes of the slice: x: 4 (x_hi: 2, x_lo: 2; x = x_hi * 2 + x_lo), y: 4, z: 8, core: 2. Of those that a mesh axis runs over, the one named last changes fastest.
Arguments:
- tokens: bfloat16 [8192, 4096], P('seq'), may hold values from -6 to 6
- in_weight: bfloat16 [4096, 3, 4096], P(None, None, 'ch'), may hold values from -0.09375 to 0.09375
- short_taps: float32 [3, 3, 4096], P(None, None, 'ch'), may hold values from -3 to 3
- band_freq: float32 [16], replicated, may hold values from 1 to 512
- filter_first: float32 [33, 64], replicated, may hold values from -6 to 6
- filter_bias: float32 [64], replicated, may hold values from -3.140625 to 3.140625
- filter_out: float32 [64, 4096], P(None, 'ch'), may hold values from -0.0234375 to 0.0234375
- decay: float32 [4096], P('ch'), may hold values from 1.2207031e-05 to 0.02
- out_weight: bfloat16 [4096, 4096], P('ch'), may hold values from -0.125 to 0.125
Outputs:
- layer_out: bfloat16 [8192, 4096], P('seq', 'ch')
The draws below stay inside these ranges and needn't reach their ends.
All inputs are finite; a program needn't handle non-finite values.
Results may differ from the reference program's by a relative error of at most 0.03.
Values may be sent and summed in bfloat16 or wider, within the bound.
A program may use at most 128 MiB of HBM per device.

```python
import math
import jax
import jax.numpy as jnp
from jax import lax

D = 4096
ORDER = 64
BANDS = 16
SHORT = 3
TOKENS = 8192
N_CH = 16


def strengthened(result, key, source, target, parts, factor):
    def block_of(dim):
        return (jnp.arange(result.shape[dim]) // (result.shape[dim] // parts)).reshape((-1,) + (1,) * (result.ndim - 1 - dim))

    one_side = jax.random.permutation(key, parts)[block_of(target)]
    other_side = (block_of(target) + parts // 2) % parts
    return jnp.where((block_of(source) == one_side) | (block_of(source) == other_side), factor * result, result)


def shard_levels(key, dims, split, low, top_value):
    def one(position, blocks):
        draws = jax.random.uniform(jax.random.fold_in(jax.random.fold_in(key, 6), position), (blocks,), jnp.float32, low / len(split), top_value / len(split))
        return jnp.repeat(jnp.exp(draws), dims[position] // blocks).reshape((-1,) + (1,) * (len(dims) - position - 1))

    loudness = one(*split[0])
    for cut in split[1:]:
        loudness = loudness * one(*cut)
    return loudness


def gaussian(key, shape, spread, bound, cuts=(), kind=jnp.bfloat16):
    array = spread * jax.random.normal(key, shape, jnp.float32)
    if cuts:
        array = array * shard_levels(key, shape, cuts, -0.22, 0.18)
    return jnp.clip(array, -bound, bound).astype(kind)


def gaussian_with(own_key, shape, width, reach, cuts, heavy, dtype=jnp.bfloat16):
    drawn = width * jax.random.normal(own_key, shape, jnp.float32)
    if cuts:
        drawn = drawn * shard_levels(own_key, shape, cuts, -0.22, 0.18)
    return jnp.clip(strengthened(drawn, jax.random.fold_in(own_key, 3), *heavy), -reach, reach).astype(dtype)


def setup_inputs(seed: int = 0) -> dict:
    keys = jax.random.split(jax.random.key(seed), 10)
    tokens = gaussian(keys[0], (TOKENS, D), 1.0, 6.0, ((0, 16),))
    in_weight = gaussian(keys[1], (D, 3, D), D ** -0.5, 0.09375, ((2, 16),))
    short_taps = gaussian(keys[2], (SHORT, 3, D), 0.6, 3.0, ((2, 16),), jnp.float32)
    band_freq = jnp.clip(jnp.exp(jax.random.uniform(keys[3], (BANDS,), jnp.float32, math.log(1.0), math.log(512.0))), 1.0, 512.0)
    filter_first = jnp.clip(jax.random.uniform(keys[4], (2 * BANDS + 1, ORDER), jnp.float32, -6.0, 6.0), -6.0, 6.0)
    filter_bias = jnp.clip(jax.random.uniform(keys[5], (ORDER,), jnp.float32, -3.140625, 3.140625), -3.140625, 3.140625)
    filter_out = gaussian(keys[6], (ORDER, D), (ORDER * TOKENS // 8) ** -0.5, 0.0234375, ((1, 16),), jnp.float32)
    decay = jnp.clip(jnp.exp(math.log(0.02) - 7.4014754 * jax.random.uniform(keys[7], (D,), jnp.float32) ** shard_levels(keys[7], (D,), ((0, 16),), -0.2, 0.2)), 1.220703143189894e-05, 0.02)
    out_weight = gaussian_with(keys[8], (D, D), D ** -0.5, 0.125, ((0, 16),), (0, 1, 16, 2.0))
    return {"tokens": tokens, "in_weight": in_weight, "short_taps": short_taps, "band_freq": band_freq, "filter_first": filter_first, "filter_bias": filter_bias, "filter_out": filter_out, "decay": decay, "out_weight": out_weight}


def filter_values(positions, seq_length, band_freq, filter_first, filter_bias, out_cols, decay_cols):
    phase = (2.0 * math.pi / seq_length) * (positions[:, None] * band_freq[None, :])
    features = jnp.concatenate([positions[:, None] / seq_length, jnp.cos(phase), jnp.sin(phase)], 1)
    filter_hidden = jnp.sin(jnp.dot(features, filter_first, precision=lax.Precision.HIGHEST) + filter_bias)
    shaped = jnp.dot(filter_hidden, out_cols, precision=lax.Precision.HIGHEST)
    return shaped * jnp.exp(-decay_cols[None, :] * positions[:, None])


def conv_block(operands):
    spectrum = jnp.fft.rfft(operands[0], 2 * TOKENS, axis=0) * jnp.fft.rfft(operands[1], 2 * TOKENS, axis=0)
    return jnp.fft.irfft(spectrum, 2 * TOKENS, axis=0)[:TOKENS]


def add_group(carry, operands):
    term = jnp.dot(operands[0], operands[1], preferred_element_type=jnp.float32).astype(jnp.bfloat16)
    term = lax.optimization_barrier(term)
    return carry + term.astype(jnp.float32), None


def reference(tokens, in_weight, short_taps, band_freq, filter_first, filter_bias, filter_out, decay, out_weight):
    projected = jnp.dot(tokens, in_weight.reshape(D, 3 * D), preferred_element_type=jnp.float32)
    projected = projected.astype(jnp.bfloat16).reshape(TOKENS, 3, D)
    padded = jnp.concatenate([jnp.zeros((SHORT - 1, 3, D), jnp.bfloat16), projected], 0).astype(jnp.float32)
    mixed_proj = short_taps[0] * padded[SHORT - 1:]
    for offset in range(1, SHORT):
        mixed_proj = mixed_proj + short_taps[offset] * padded[SHORT - 1 - offset:SHORT - 1 - offset + TOKENS]
    source = mixed_proj[:, 0] * mixed_proj[:, 2]
    positions = lax.iota(jnp.int32, TOKENS).astype(jnp.float32)
    impulse = filter_values(positions, TOKENS, band_freq, filter_first, filter_bias, filter_out, decay)
    block_width = min(D, 256)
    block_count = D // block_width
    source_blocks = source.reshape(TOKENS, block_count, block_width).transpose(1, 0, 2)
    impulse_blocks = impulse.reshape(TOKENS, block_count, block_width).transpose(1, 0, 2)
    conv = lax.map(conv_block, (source_blocks, impulse_blocks))
    conv = conv.transpose(1, 0, 2).reshape(TOKENS, D)
    gated = (mixed_proj[:, 1] * conv).astype(jnp.bfloat16)
    gated_groups = gated.reshape(TOKENS, N_CH, D // N_CH).transpose(1, 0, 2)
    weight_groups = out_weight.reshape(N_CH, D // N_CH, D)
    summed, ignored = lax.scan(add_group, jnp.zeros((TOKENS, D), jnp.float32), (gated_groups, weight_groups))
    return summed.astype(jnp.bfloat16)
```

```python
import functools
import math

import jax
import jax.numpy as jnp
import numpy as np
from jax import lax
from jax.experimental import pallas as pl
from jax.experimental.pallas import tpu as pltpu
from jax.sharding import PartitionSpec as P

MESH = pl.DeviceIdType.MESH
BF = jnp.bfloat16
F32 = jnp.float32
HIGH = lax.Precision.HIGHEST
RADIX = 128
HALF = 80


def dft_tables(rows_in):
    full = RADIX * RADIX
    k1 = np.arange(HALF)[:, None]
    used = (k1 <= RADIX // 2).astype(np.float64)
    line = np.arange(RADIX)
    a = 2 * np.pi * k1 * np.arange(rows_in)[None, :] / RADIX
    outer = np.concatenate([np.cos(a) * used, -np.sin(a) * used], 0)
    tw = 2 * np.pi * k1 * line[None, :] / full
    twist = np.stack([np.cos(tw), np.sin(tw)])
    b = 2 * np.pi * np.outer(line, line) / RADIX
    co, si = np.cos(b), np.sin(b)
    inner = np.block([[co, -si], [si, co]])
    inner_back = np.block([[co, si], [-si, co]])
    weight = np.where((k1 == 0) | (k1 == RADIX // 2), 1.0, 2.0) * used / full
    outer_back = np.concatenate([(np.cos(a) * weight).T, (-np.sin(a) * weight).T], 1)
    return (
        jnp.asarray(outer, BF),
        jnp.asarray(twist, F32),
        jnp.asarray(inner, BF),
        jnp.asarray(inner_back, BF),
        jnp.asarray(outer_back, BF),
    )


def sin_turns(turns):
    turns = turns - 0.25
    turns = turns - jnp.round(turns)
    x = (0.25 - jnp.abs(turns)) * (2.0 * math.pi)
    x2 = x * x
    p = jnp.float32(-2.50521083854e-8)
    for c in (2.75573192239858e-6, -1.98412698412698e-4, 8.33333333333333e-3, -1.66666666666667e-1):
        p = p * x2 + jnp.float32(c)
    return x + x * x2 * p


def first_row(v):
    row = lax.broadcasted_iota(jnp.int32, (8, v.shape[1]), 0)
    return jnp.where(row == 0, jnp.broadcast_to(v, (8, v.shape[1])), 0.0)


def contract_rows(a, b):
    return lax.dot_general(a, b, (((0,), (0,)), ((), ())), precision=HIGH, preferred_element_type=F32)


def outer_product(v, w):
    return contract_rows(first_row(v), first_row(w))


def forward(grid32, x_all, a_all, rows_all, outer, twist, inner, spec_ref, channels):
    rows_in = x_all.shape[0]
    for c in range(channels):
        x_all[:, c * RADIX : (c + 1) * RADIX] = grid32[pl.ds(c, rows_in, stride=channels), :].astype(BF)
    a_all[...] = jnp.dot(outer[...], x_all[...], preferred_element_type=F32)
    co, si = twist[0], twist[1]
    for c in range(channels):
        lanes = slice(c * RADIX, (c + 1) * RADIX)
        re, im = a_all[:HALF, lanes], a_all[HALF:, lanes]
        rows = slice(c * HALF, (c + 1) * HALF)
        rows_all[rows, :RADIX] = (re * co + im * si).astype(BF)
        rows_all[rows, RADIX:] = (im * co - re * si).astype(BF)
    spec_ref[...] = jnp.dot(rows_all[...], inner[...], preferred_element_type=F32)


def operator_kernel(
    n_seq,
    tok_hbm, w_hbm, taps, band, first, bias, fout, decay, outer_hbm, twist_hbm, inner_hbm, inner_back_hbm, outer_back_hbm,
    gated_ref,
    tok, w, outer, twist, inner, inner_back, outer_back,
    px, gate, halo_s, halo_r, send4, imp4, imp_recv, src_recv, conv_send, conv4,
    grid32, x_all, a_all, rows_all, imp_spec, src_spec,
    load_sem, halo_sem, imp_ssem, imp_rsem, src_ssem, src_rsem, conv_ssem, conv_rsem, own_sem,
):
    me = lax.axis_index("seq")
    rows, width = tok_hbm.shape
    slab = w_hbm.shape[2]
    channels = slab // n_seq
    per = rows // RADIX
    half = rows // 2
    length = rows * n_seq

    loads = [
        pltpu.make_async_copy(w_hbm.at[0], w.at[0], load_sem.at[0]),
        pltpu.make_async_copy(w_hbm.at[2], w.at[2], load_sem.at[1]),
        pltpu.make_async_copy(tok_hbm.at[half:], tok.at[half:], load_sem.at[2]),
        pltpu.make_async_copy(tok_hbm.at[:half], tok.at[:half], load_sem.at[3]),
        pltpu.make_async_copy(w_hbm.at[1], w.at[1], load_sem.at[4]),
        pltpu.make_async_copy(outer_hbm, outer, load_sem.at[5]),
        pltpu.make_async_copy(twist_hbm, twist, load_sem.at[6]),
        pltpu.make_async_copy(inner_hbm, inner, load_sem.at[7]),
        pltpu.make_async_copy(inner_back_hbm, inner_back, load_sem.at[8]),
        pltpu.make_async_copy(outer_back_hbm, outer_back, load_sem.at[9]),
    ]
    for copy in loads:
        copy.start()

    barrier = pltpu.get_barrier_semaphore()

    def greet(d, carry):
        pl.semaphore_signal(barrier, inc=1, device_id={"seq": lax.rem(me + d, n_seq)}, device_id_type=MESH)
        return carry

    lax.fori_loop(1, n_seq, greet, 0)

    pos = (me * rows + lax.broadcasted_iota(jnp.int32, (1, rows), 1)).astype(F32)
    scaled = pos * (1.0 / length)
    turns = outer_product(band[...], scaled)
    turns = turns - jnp.round(turns)
    n_band = band.shape[1]
    head = lax.broadcasted_iota(jnp.int32, (8, rows), 0)
    features = jnp.concatenate(
        [sin_turns(turns + 0.25), sin_turns(turns), jnp.where(head == 0, scaled, jnp.where(head == 1, 1.0, 0.0))], 0
    )
    head = lax.broadcasted_iota(jnp.int32, (8, first.shape[1]), 0)
    layer = jnp.concatenate(
        [
            first[1 : 1 + n_band, :],
            first[1 + n_band :, :],
            jnp.where(head == 0, first[0:1, :], jnp.where(head == 1, bias[...], 0.0)),
        ],
        0,
    )
    pre = contract_rows(layer, features)
    hidden = sin_turns(pre * (1.0 / (2.0 * math.pi)))
    impulse = contract_rows(fout[...], hidden) * jnp.exp(-outer_product(decay[...], pos))
    for q in range(per):
        imp4[q] = impulse[:, q * RADIX : (q + 1) * RADIX].astype(BF)

    pl.semaphore_wait(barrier, n_seq - 1)

    def spread_copy(src, dst, ssem, rsem, peer):
        return pltpu.make_async_remote_copy(
            src_ref=src.at[:, pl.ds(pl.multiple_of(peer * channels, channels), channels), :],
            dst_ref=dst.at[pl.ds(me * per, per)],
            send_sem=ssem.at[peer],
            recv_sem=rsem.at[me],
            device_id={"seq": peer},
            device_id_type=MESH,
        )

    def arrive(dst, ssem, rsem, peer):
        return pltpu.make_async_remote_copy(
            src_ref=dst.at[pl.ds(peer * per, per)],
            dst_ref=dst.at[pl.ds(peer * per, per)],
            send_sem=ssem.at[peer],
            recv_sem=rsem.at[peer],
            device_id={"seq": peer},
            device_id_type=MESH,
        )

    def own_piece(src, dst):
        dst[pl.ds(me * per, per)] = src[:, pl.ds(pl.multiple_of(me * channels, channels), channels), :]

    def each_peer(step):
        def body(d, carry):
            step(lax.rem(me + d, n_seq))
            return carry

        lax.fori_loop(1, n_seq, body, 0)

    each_peer(lambda p: spread_copy(imp4, imp_recv, imp_ssem, imp_rsem, p).start())
    own_piece(imp4, imp_recv)

    after = lax.rem(me + 1, n_seq)
    before = lax.rem(me + n_seq - 1, n_seq)

    def halo_copy(g):
        return pltpu.make_async_remote_copy(
            src_ref=halo_s.at[g], dst_ref=halo_r.at[g], send_sem=halo_sem.at[0, g], recv_sem=halo_sem.at[1, g],
            device_id={"seq": after}, device_id_type=MESH,
        )

    def project(g, part):
        out = jnp.dot(tok[part * half : (part + 1) * half, :], w[g], preferred_element_type=F32).astype(BF)
        px[g, 16 + part * half : 16 + (part + 1) * half, :] = out.astype(F32)
        if part == 1:
            halo_s[g] = out[half - 16 :, :]
            halo_copy(g).start()

    def take_halo(g):
        halo_copy(g).wait()
        px[g, 0:16, :] = jnp.where(me > 0, halo_r[g].astype(F32), 0.0)

    def mixed(g, q):
        total = taps[0, g : g + 1, :] * px[g, 16 + q * RADIX : 16 + (q + 1) * RADIX, :]
        for i in (1, 2):
            total = total + taps[i, g : g + 1, :] * px[g, 16 - i + q * RADIX : 16 - i + (q + 1) * RADIX, :]
        return total

    loads[0].wait()
    loads[1].wait()
    loads[2].wait()
    project(0, 1)
    project(2, 1)
    loads[3].wait()
    project(0, 0)
    project(2, 0)
    take_halo(0)
    take_halo(2)
    for q in range(per):
        send4[q] = (mixed(0, q) * mixed(2, q)).T.astype(BF)
    each_peer(lambda p: spread_copy(send4, src_recv, src_ssem, src_rsem, p).start())
    own_piece(send4, src_recv)

    loads[4].wait()
    project(1, 1)
    project(1, 0)
    take_halo(1)
    for q in range(per):
        gate[q * RADIX : (q + 1) * RADIX, :] = mixed(1, q)

    for copy in loads[5:]:
        copy.wait()
    each_peer(lambda p: arrive(imp_recv, imp_ssem, imp_rsem, p).wait_recv())
    points = per * n_seq
    grid32[...] = imp_recv[...].astype(F32).reshape(points * channels, RADIX)
    forward(grid32, x_all, a_all, rows_all, outer, twist, inner, imp_spec, channels)

    each_peer(lambda p: arrive(src_recv, src_ssem, src_rsem, p).wait_recv())
    grid32[...] = src_recv[...].astype(F32).reshape(points * channels, RADIX)
    forward(grid32, x_all, a_all, rows_all, outer, twist, inner, src_spec, channels)

    for c in range(channels):
        line = slice(c * HALF, (c + 1) * HALF)
        sre, sim = src_spec[line, :RADIX], src_spec[line, RADIX:]
        ire, iim = imp_spec[line, :RADIX], imp_spec[line, RADIX:]
        rows_all[line, :RADIX] = (sre * ire - sim * iim).astype(BF)
        rows_all[line, RADIX:] = (sre * iim + sim * ire).astype(BF)
    src_spec[...] = jnp.dot(rows_all[...], inner_back[...], preferred_element_type=F32)
    co, si = twist[0], twist[1]
    for c in range(channels):
        line = slice(c * HALF, (c + 1) * HALF)
        lanes = slice(c * RADIX, (c + 1) * RADIX)
        re, im = src_spec[line, :RADIX], src_spec[line, RADIX:]
        back = jnp.concatenate([re * co - im * si, im * co + re * si], 0).astype(BF)
        y = jnp.dot(outer_back[...], back, preferred_element_type=F32)
        grid32[pl.ds(c, points, stride=channels), :] = y
    conv_send[...] = grid32[...].astype(BF).reshape(points, channels, RADIX)

    def return_copy(peer):
        return pltpu.make_async_remote_copy(
            src_ref=conv_send.at[pl.ds(peer * per, per)],
            dst_ref=conv4.at[:, pl.ds(pl.multiple_of(me * channels, channels), channels), :],
            send_sem=conv_ssem.at[peer],
            recv_sem=conv_rsem.at[me],
            device_id={"seq": peer},
            device_id_type=MESH,
        )

    def return_arrive(peer):
        piece = conv4.at[:, pl.ds(pl.multiple_of(peer * channels, channels), channels), :]
        return pltpu.make_async_remote_copy(
            src_ref=piece, dst_ref=piece, send_sem=conv_ssem.at[peer], recv_sem=conv_rsem.at[peer],
            device_id={"seq": peer}, device_id_type=MESH,
        )

    each_peer(lambda p: return_copy(p).start())
    conv4[:, pl.ds(pl.multiple_of(me * channels, channels), channels), :] = conv_send[pl.ds(me * per, per)]
    each_peer(lambda p: return_arrive(p).wait_recv())
    for q in range(per):
        line = slice(q * RADIX, (q + 1) * RADIX)
        gated_ref[line, :] = (gate[line, :] * conv4[q].astype(F32).T).astype(BF)

    each_peer(lambda p: spread_copy(imp4, imp_recv, imp_ssem, imp_rsem, p).wait_send())
    each_peer(lambda p: spread_copy(send4, src_recv, src_ssem, src_rsem, p).wait_send())
    each_peer(lambda p: return_copy(p).wait_send())


def gated_rows(n_seq, tokens, in_weight, short_taps, band_freq, filter_first, filter_bias, filter_out, decay):
    rows, width = tokens.shape
    slab = in_weight.shape[2]
    channels = slab // n_seq
    per = rows // RADIX
    points = per * n_seq
    tables = dft_tables(points)
    anyspec = pl.BlockSpec(memory_space=pl.ANY)
    vspec = pl.BlockSpec(memory_space=pltpu.VMEM)
    dma = pltpu.SemaphoreType.DMA
    scratch = [
        pltpu.VMEM((rows, width), BF),
        pltpu.VMEM((3, width, slab), BF),
        *[pltpu.VMEM(t.shape, t.dtype) for t in tables],
        pltpu.VMEM((3, rows + 16, slab), F32),
        pltpu.VMEM((rows, slab), F32),
        pltpu.VMEM((3, 16, slab), BF),
        pltpu.VMEM((3, 16, slab), BF),
        pltpu.VMEM((per, slab, RADIX), BF),
        pltpu.VMEM((per, slab, RADIX), BF),
        pltpu.VMEM((points, channels, RADIX), BF),
        pltpu.VMEM((points, channels, RADIX), BF),
        pltpu.VMEM((points, channels, RADIX), BF),
        pltpu.VMEM((per, slab, RADIX), BF),
        pltpu.VMEM((points * channels, RADIX), F32),
        pltpu.VMEM((points, channels * RADIX), BF),
        pltpu.VMEM((2 * HALF, channels * RADIX), F32),
        pltpu.VMEM((channels * HALF, 2 * RADIX), BF),
        pltpu.VMEM((channels * HALF, 2 * RADIX), F32),
        pltpu.VMEM((channels * HALF, 2 * RADIX), F32),
        dma((10,)), dma((2, 3)), dma((n_seq,)), dma((n_seq,)), dma((n_seq,)), dma((n_seq,)), dma((n_seq,)), dma((n_seq,)), dma,
    ]
    return pl.pallas_call(
        functools.partial(operator_kernel, n_seq),
        out_shape=jax.ShapeDtypeStruct((rows, slab), BF),
        in_specs=[anyspec] * 2 + [vspec] * 6 + [anyspec] * 5,
        out_specs=vspec,
        scratch_shapes=scratch,
        compiler_params=pltpu.CompilerParams(collective_id=0, has_side_effects=True, vmem_limit_bytes=56 * 2**20),
        cost_estimate=pl.CostEstimate(flops=2 * rows * width * slab * 3, bytes_accessed=12 * 2**20, transcendentals=0),
    )(
        tokens, jnp.transpose(in_weight, (1, 0, 2)), short_taps, band_freq[None, :], filter_first, filter_bias[None, :],
        filter_out, decay[None, :], *tables,
    )


def local(tokens, in_weight, short_taps, band_freq, filter_first, filter_bias, filter_out, decay, out_weight):
    gated_out = gated_rows(
        lax.axis_size("seq"), tokens, in_weight, short_taps, band_freq, filter_first, filter_bias, filter_out, decay
    )
    summed = lax.psum_scatter(
        lax.dot_general(
            out_weight, gated_out, (((0,), (1,)), ((), ())), preferred_element_type=jnp.float32
        ).astype(jnp.bfloat16),
        "ch",
        scatter_dimension=0,
        tiled=True,
    ).astype(jnp.float32)
    return summed.T.astype(jnp.bfloat16)


def solution(mesh):
    in_specs = (
        P("seq", None),
        P(None, None, "ch"),
        P(None, None, "ch"),
        P(),
        P(),
        P(),
        P(None, "ch"),
        P("ch"),
        P("ch", None),
    )
    out_specs = P("seq", "ch")
    return jax.shard_map(local, mesh=mesh, in_specs=in_specs, out_specs=out_specs, check_vma=False)
```

```python
import functools
import math

import jax
import jax.numpy as jnp
import numpy as np
from jax import lax
from jax.experimental import pallas as pl
from jax.experimental.pallas import tpu as pltpu
from jax.sharding import PartitionSpec as P

MESH = pl.DeviceIdType.MESH
BF = jnp.bfloat16
F32 = jnp.float32
HIGH = lax.Precision.HIGHEST
RADIX = 128
HALF = 80


def dft_tables(rows_in):
    full = RADIX * RADIX
    k1 = np.arange(HALF)[:, None]
    used = (k1 <= RADIX // 2).astype(np.float64)
    line = np.arange(RADIX)
    a = 2 * np.pi * k1 * np.arange(rows_in)[None, :] / RADIX
    outer = np.concatenate([np.cos(a) * used, -np.sin(a) * used], 0)
    tw = 2 * np.pi * k1 * line[None, :] / full
    twist = np.stack([np.cos(tw), np.sin(tw)])
    b = 2 * np.pi * np.outer(line, line) / RADIX
    co, si = np.cos(b), np.sin(b)
    inner = np.block([[co, -si], [si, co]])
    inner_back = np.block([[co, si], [-si, co]])
    weight = np.where((k1 == 0) | (k1 == RADIX // 2), 1.0, 2.0) * used / full
    outer_back = np.concatenate([(np.cos(a) * weight).T, (-np.sin(a) * weight).T], 1)
    return (
        jnp.asarray(outer, BF),
        jnp.asarray(twist, F32),
        jnp.asarray(inner, BF),
        jnp.asarray(inner_back, BF),
        jnp.asarray(outer_back, BF),
    )


def sin_turns(turns):
    turns = turns - 0.25
    turns = turns - jnp.round(turns)
    x = (0.25 - jnp.abs(turns)) * (2.0 * math.pi)
    x2 = x * x
    p = jnp.float32(-2.50521083854e-8)
    for c in (2.75573192239858e-6, -1.98412698412698e-4, 8.33333333333333e-3, -1.66666666666667e-1):
        p = p * x2 + jnp.float32(c)
    return x + x * x2 * p


def first_row(v):
    row = lax.broadcasted_iota(jnp.int32, (8, v.shape[1]), 0)
    return jnp.where(row == 0, jnp.broadcast_to(v, (8, v.shape[1])), 0.0)


def contract_rows(a, b):
    return lax.dot_general(a, b, (((0,), (0,)), ((), ())), precision=HIGH, preferred_element_type=F32)


def outer_product(v, w):
    return contract_rows(first_row(v), first_row(w))


def forward(grid32, x_all, a_all, rows_all, outer, twist, inner, spec_ref, channels):
    rows_in = x_all.shape[0]
    for c in range(channels):
        x_all[:, c * RADIX : (c + 1) * RADIX] = grid32[pl.ds(c, rows_in, stride=channels), :].astype(BF)
    a_all[...] = jnp.dot(outer[...], x_all[...], preferred_element_type=F32)
    co, si = twist[0], twist[1]
    for c in range(channels):
        lanes = slice(c * RADIX, (c + 1) * RADIX)
        re, im = a_all[:HALF, lanes], a_all[HALF:, lanes]
        rows = slice(c * HALF, (c + 1) * HALF)
        rows_all[rows, :RADIX] = (re * co + im * si).astype(BF)
        rows_all[rows, RADIX:] = (im * co - re * si).astype(BF)
    spec_ref[...] = jnp.dot(rows_all[...], inner[...], preferred_element_type=F32)


CHUNK = 64


class Spread:
    def __init__(self, n_ch, w_hbm, out_ref, wout, g2, sums, landed, wl_sem, wx_ssem, wx_rsem, wc_sem, gx_ssem, gx_rsem, r_ssem, r_rsem):
        self.__dict__.update(locals())
        del self.__dict__["self"]
        self.n_z = n_ch // 2
        self.c = lax.axis_index("ch")
        self.z = self.c // 2
        self.xl = lax.rem(self.c, 2)
        self.s = lax.axis_index("seq")
        self.core = lax.rem(self.s, 2)
        self.partner = {"ch": self.c + 1 - 2 * self.xl}
        self.sibling = {"seq": self.s + 1 - 2 * self.core}
        self.up = {"ch": lax.rem(self.c + 2, n_ch)}
        self.down = {"ch": lax.rem(self.c + n_ch - 2, n_ch)}
        self.depth = w_hbm.shape[0]
        self.cols = w_hbm.shape[1] // n_ch
        self.rows = out_ref.shape[0]
        self.chunks = self.rows // CHUNK

    def peers(self):
        return [self.partner, self.up, self.down]

    def _columns(self, block):
        return pl.ds(pl.multiple_of(block * self.cols, self.cols), self.cols)

    def own_weight(self, j):
        return pltpu.make_async_copy(
            self.w_hbm.at[:, self._columns(2 * j + self.xl)], self.wout.at[0, j], self.wl_sem.at[j]
        )

    def weight_to_partner(self, j):
        half = self.depth // 2
        part = pl.ds(pl.multiple_of(self.core * half, half), half)
        return pltpu.make_async_remote_copy(
            src_ref=self.w_hbm.at[part, self._columns(2 * j + 1 - self.xl)],
            dst_ref=self.wout.at[1, j, part, :],
            send_sem=self.wx_ssem.at[j], recv_sem=self.wx_rsem.at[j], device_id=self.partner, device_id_type=MESH,
        )

    def weight_to_sibling(self):
        half = self.depth // 2
        part = pl.ds(pl.multiple_of(self.core * half, half), half)
        return pltpu.make_async_remote_copy(
            src_ref=self.wout.at[1, :, part, :], dst_ref=self.wout.at[1, :, part, :],
            send_sem=self.wc_sem.at[0], recv_sem=self.wc_sem.at[1], device_id=self.sibling, device_id_type=MESH,
        )

    def weight_from_sibling(self):
        half = self.depth // 2
        part = pl.ds(pl.multiple_of((1 - self.core) * half, half), half)
        return pltpu.make_async_remote_copy(
            src_ref=self.wout.at[1, :, part, :], dst_ref=self.wout.at[1, :, part, :],
            send_sem=self.wc_sem.at[0], recv_sem=self.wc_sem.at[1], device_id=self.sibling, device_id_type=MESH,
        )

    def start_weights(self):
        for j in range(self.n_z):
            self.weight_to_partner(j).start()

    def load_weights(self):
        for j in range(self.n_z):
            self.own_weight(j).start()

    def pass_weights(self):
        for j in range(self.n_z):
            self.weight_to_partner(j).wait()
        self.weight_to_sibling().start()

    def gated_to_partner(self, q):
        line = slice(q * RADIX, (q + 1) * RADIX)
        return pltpu.make_async_remote_copy(
            src_ref=self.g2.at[0, line], dst_ref=self.g2.at[1, line],
            send_sem=self.gx_ssem.at[q], recv_sem=self.gx_rsem.at[q], device_id=self.partner, device_id_type=MESH,
        )

    def hop(self, way, step, i):
        return pltpu.make_async_remote_copy(
            src_ref=self.sums.at[way, step, i], dst_ref=self.landed.at[way, step, i],
            send_sem=self.r_ssem.at[way, step, i], recv_sem=self.r_rsem.at[way, step, i],
            device_id=(self.up, self.down)[way], device_id_type=MESH,
        )

    def partial_sum(self, block, i):
        line = pl.ds(pl.multiple_of(i * CHUNK, CHUNK), CHUNK)
        return jnp.dot(self.g2[0, line], self.wout[0, block], preferred_element_type=F32) + jnp.dot(
            self.g2[1, line], self.wout[1, block], preferred_element_type=F32
        )

    def block_at(self, way, step):
        n = self.n_z
        if way == 0:
            return lax.rem(self.z + n // 2 - step, n)
        return lax.rem(self.z + n // 2 + step, n)

    def send(self, way, step, i, fresh):
        own = self.partial_sum(self.block_at(way, step), i)
        if not fresh:
            self.hop(way, step - 1, i).wait_recv()
            own = own + self.landed[way, step - 1, i].astype(F32)
        self.sums[way, step, i] = own.astype(BF)
        self.hop(way, step, i).start()

    def finish(self, per):
        for j in range(self.n_z):
            self.own_weight(j).wait()
        self.weight_to_sibling().wait_send()
        self.weight_from_sibling().wait_recv()
        half = self.chunks // 2
        for q in range(per):
            self.gated_to_partner(q).wait_recv()

        def both(step, first, fresh):
            def body(i, carry):
                self.send(0, step, i if first else half + i, fresh)
                self.send(1, step, half + i if first else i, fresh)
                return carry

            lax.fori_loop(0, half, body, 0)

        both(0, True, True)
        both(1, False, True)
        both(1, True, False)
        steps = self.n_z // 2
        for step in range(2, steps):
            both(step, False, False)
            both(step, True, False)

        def home(i, carry):
            own = self.partial_sum(self.z, i)
            self.hop(0, steps - 1, i).wait_recv()
            self.hop(1, steps - 1, i).wait_recv()
            own = own + self.landed[0, steps - 1, i].astype(F32) + self.landed[1, steps - 1, i].astype(F32)
            self.out_ref[pl.ds(pl.multiple_of(i * CHUNK, CHUNK), CHUNK), :] = own.astype(BF)
            return carry

        lax.fori_loop(0, self.chunks, home, 0)

        for q in range(per):
            self.gated_to_partner(q).wait_send()

        def drain(i, carry):
            for step in range(1, steps):
                self.hop(0, step, i).wait_send()
                self.hop(1, step, i).wait_send()
            return carry

        lax.fori_loop(0, self.chunks, drain, 0)

        def drain_first(i, carry):
            self.hop(0, 0, i).wait_send()
            self.hop(1, 0, half + i).wait_send()
            return carry

        lax.fori_loop(0, half, drain_first, 0)


def spread_scratch(n_ch, rows, depth, cols, per):
    n_z = n_ch // 2
    dma = pltpu.SemaphoreType.DMA
    return [
        pltpu.VMEM((2, n_z, depth, cols), BF),
        pltpu.VMEM((2, rows, depth), BF),
        pltpu.VMEM((2, n_z // 2, rows // CHUNK, CHUNK, cols), BF),
        pltpu.VMEM((2, n_z // 2, rows // CHUNK, CHUNK, cols), BF),
        dma((n_z,)), dma((n_z,)), dma((n_z,)), dma((2,)), dma((per,)), dma((per,)),
        dma((2, n_z // 2, rows // CHUNK)), dma((2, n_z // 2, rows // CHUNK)),
    ]


def operator_kernel(
    n_seq, n_ch,
    tok_hbm, w_hbm, taps, band, first, bias, fout, decay, outer_hbm, twist_hbm, inner_hbm, inner_back_hbm, outer_back_hbm, wout_hbm,
    out_ref,
    tok, w, outer, twist, inner, inner_back, outer_back,
    px, gate, halo_s, halo_r, send4, imp4, imp_recv, src_recv, conv_send, conv4,
    grid32, x_all, a_all, rows_all, imp_spec, src_spec,
    load_sem, halo_sem, imp_ssem, imp_rsem, src_ssem, src_rsem, conv_ssem, conv_rsem, *out_scratch,
):
    me = lax.axis_index("seq")
    out = Spread(n_ch, wout_hbm, out_ref, *out_scratch)
    rows, width = tok_hbm.shape
    slab = w_hbm.shape[2]
    channels = slab // n_seq
    per = rows // RADIX
    half = rows // 2
    length = rows * n_seq

    loads = [
        pltpu.make_async_copy(w_hbm.at[0], w.at[0], load_sem.at[0]),
        pltpu.make_async_copy(w_hbm.at[2], w.at[2], load_sem.at[1]),
        pltpu.make_async_copy(tok_hbm.at[half:], tok.at[half:], load_sem.at[2]),
        pltpu.make_async_copy(tok_hbm.at[:half], tok.at[:half], load_sem.at[3]),
        pltpu.make_async_copy(w_hbm.at[1], w.at[1], load_sem.at[4]),
        pltpu.make_async_copy(outer_hbm, outer, load_sem.at[5]),
        pltpu.make_async_copy(twist_hbm, twist, load_sem.at[6]),
        pltpu.make_async_copy(inner_hbm, inner, load_sem.at[7]),
        pltpu.make_async_copy(inner_back_hbm, inner_back, load_sem.at[8]),
        pltpu.make_async_copy(outer_back_hbm, outer_back, load_sem.at[9]),
    ]
    for copy in loads:
        copy.start()
    out.load_weights()

    barrier = pltpu.get_barrier_semaphore()

    def greet(d, carry):
        pl.semaphore_signal(barrier, inc=1, device_id={"seq": lax.rem(me + d, n_seq)}, device_id_type=MESH)
        return carry

    lax.fori_loop(1, n_seq, greet, 0)
    for peer in out.peers():
        pl.semaphore_signal(barrier, inc=1, device_id=peer, device_id_type=MESH)

    pos = (me * rows + lax.broadcasted_iota(jnp.int32, (1, rows), 1)).astype(F32)
    scaled = pos * (1.0 / length)
    turns = outer_product(band[...], scaled)
    turns = turns - jnp.round(turns)
    n_band = band.shape[1]
    head = lax.broadcasted_iota(jnp.int32, (8, rows), 0)
    features = jnp.concatenate(
        [sin_turns(turns + 0.25), sin_turns(turns), jnp.where(head == 0, scaled, jnp.where(head == 1, 1.0, 0.0))], 0
    )
    head = lax.broadcasted_iota(jnp.int32, (8, first.shape[1]), 0)
    layer = jnp.concatenate(
        [
            first[1 : 1 + n_band, :],
            first[1 + n_band :, :],
            jnp.where(head == 0, first[0:1, :], jnp.where(head == 1, bias[...], 0.0)),
        ],
        0,
    )
    pre = contract_rows(layer, features)
    hidden = sin_turns(pre * (1.0 / (2.0 * math.pi)))
    impulse = contract_rows(fout[...], hidden) * jnp.exp(-outer_product(decay[...], pos))
    for q in range(per):
        imp4[q] = impulse[:, q * RADIX : (q + 1) * RADIX].astype(BF)

    def spread_copy(src, dst, ssem, rsem, peer):
        return pltpu.make_async_remote_copy(
            src_ref=src.at[:, pl.ds(pl.multiple_of(peer * channels, channels), channels), :],
            dst_ref=dst.at[pl.ds(me * per, per)],
            send_sem=ssem.at[peer],
            recv_sem=rsem.at[me],
            device_id={"seq": peer},
            device_id_type=MESH,
        )

    def arrive(dst, ssem, rsem, peer):
        return pltpu.make_async_remote_copy(
            src_ref=dst.at[pl.ds(peer * per, per)],
            dst_ref=dst.at[pl.ds(peer * per, per)],
            send_sem=ssem.at[peer],
            recv_sem=rsem.at[peer],
            device_id={"seq": peer},
            device_id_type=MESH,
        )

    def own_piece(src, dst):
        dst[pl.ds(me * per, per)] = src[:, pl.ds(pl.multiple_of(me * channels, channels), channels), :]

    def each_peer(step):
        def body(d, carry):
            step(lax.rem(me + d, n_seq))
            return carry

        lax.fori_loop(1, n_seq, body, 0)

    after = lax.rem(me + 1, n_seq)
    before = lax.rem(me + n_seq - 1, n_seq)

    def halo_copy(g):
        return pltpu.make_async_remote_copy(
            src_ref=halo_s.at[g], dst_ref=halo_r.at[g], send_sem=halo_sem.at[0, g], recv_sem=halo_sem.at[1, g],
            device_id={"seq": after}, device_id_type=MESH,
        )

    def project(g, part):
        y = jnp.dot(tok[part * half : (part + 1) * half, :], w[g], preferred_element_type=F32).astype(BF)
        px[g, 16 + part * half : 16 + (part + 1) * half, :] = y.astype(F32)
        if part == 1:
            halo_s[g] = y[half - 16 :, :]

    def take_halo(g):
        halo_copy(g).wait()
        px[g, 0:16, :] = jnp.where(me > 0, halo_r[g].astype(F32), 0.0)

    def mixed(g, q):
        total = taps[0, g : g + 1, :] * px[g, 16 + q * RADIX : 16 + (q + 1) * RADIX, :]
        for i in (1, 2):
            total = total + taps[i, g : g + 1, :] * px[g, 16 - i + q * RADIX : 16 - i + (q + 1) * RADIX, :]
        return total

    loads[0].wait()
    loads[1].wait()
    loads[2].wait()
    project(0, 1)
    project(2, 1)
    pl.semaphore_wait(barrier, n_seq + 2)
    halo_copy(0).start()
    halo_copy(2).start()
    each_peer(lambda p: spread_copy(imp4, imp_recv, imp_ssem, imp_rsem, p).start())
    own_piece(imp4, imp_recv)
    out.start_weights()
    loads[3].wait()
    project(0, 0)
    project(2, 0)
    loads[4].wait()
    project(1, 1)
    halo_copy(1).start()
    project(1, 0)
    take_halo(0)
    take_halo(2)
    for q in range(per):
        send4[q] = (mixed(0, q) * mixed(2, q)).T.astype(BF)
    each_peer(lambda p: spread_copy(send4, src_recv, src_ssem, src_rsem, p).start())
    own_piece(send4, src_recv)

    take_halo(1)
    for q in range(per):
        gate[q * RADIX : (q + 1) * RADIX, :] = mixed(1, q)

    for copy in loads[5:]:
        copy.wait()
    each_peer(lambda p: arrive(imp_recv, imp_ssem, imp_rsem, p).wait_recv())
    points = per * n_seq
    grid32[...] = imp_recv[...].astype(F32).reshape(points * channels, RADIX)
    forward(grid32, x_all, a_all, rows_all, outer, twist, inner, imp_spec, channels)

    each_peer(lambda p: arrive(src_recv, src_ssem, src_rsem, p).wait_recv())
    grid32[...] = src_recv[...].astype(F32).reshape(points * channels, RADIX)
    forward(grid32, x_all, a_all, rows_all, outer, twist, inner, src_spec, channels)

    for c in range(channels):
        line = slice(c * HALF, (c + 1) * HALF)
        sre, sim = src_spec[line, :RADIX], src_spec[line, RADIX:]
        ire, iim = imp_spec[line, :RADIX], imp_spec[line, RADIX:]
        rows_all[line, :RADIX] = (sre * ire - sim * iim).astype(BF)
        rows_all[line, RADIX:] = (sre * iim + sim * ire).astype(BF)
    src_spec[...] = jnp.dot(rows_all[...], inner_back[...], preferred_element_type=F32)
    co, si = twist[0], twist[1]
    for c in range(channels):
        line = slice(c * HALF, (c + 1) * HALF)
        lanes = slice(c * RADIX, (c + 1) * RADIX)
        re, im = src_spec[line, :RADIX], src_spec[line, RADIX:]
        back = jnp.concatenate([re * co - im * si, im * co + re * si], 0).astype(BF)
        y = jnp.dot(outer_back[...], back, preferred_element_type=F32)
        grid32[pl.ds(c, points, stride=channels), :] = y
    conv_send[...] = grid32[...].astype(BF).reshape(points, channels, RADIX)

    def return_copy(peer):
        return pltpu.make_async_remote_copy(
            src_ref=conv_send.at[pl.ds(peer * per, per)],
            dst_ref=conv4.at[:, pl.ds(pl.multiple_of(me * channels, channels), channels), :],
            send_sem=conv_ssem.at[peer],
            recv_sem=conv_rsem.at[me],
            device_id={"seq": peer},
            device_id_type=MESH,
        )

    def return_arrive(peer):
        piece = conv4.at[:, pl.ds(pl.multiple_of(peer * channels, channels), channels), :]
        return pltpu.make_async_remote_copy(
            src_ref=piece, dst_ref=piece, send_sem=conv_ssem.at[peer], recv_sem=conv_rsem.at[peer],
            device_id={"seq": peer}, device_id_type=MESH,
        )

    each_peer(lambda p: return_copy(p).start())
    conv4[:, pl.ds(pl.multiple_of(me * channels, channels), channels), :] = conv_send[pl.ds(me * per, per)]
    out.pass_weights()
    each_peer(lambda p: return_arrive(p).wait_recv())
    for q in range(per):
        line = slice(q * RADIX, (q + 1) * RADIX)
        out.g2[0, line] = (gate[line, :] * conv4[q].astype(F32).T).astype(BF)
        out.gated_to_partner(q).start()
    out.finish(per)

    each_peer(lambda p: spread_copy(imp4, imp_recv, imp_ssem, imp_rsem, p).wait_send())
    each_peer(lambda p: spread_copy(send4, src_recv, src_ssem, src_rsem, p).wait_send())
    each_peer(lambda p: return_copy(p).wait_send())


def operator_rows(
    n_seq, n_ch, tokens, in_weight, short_taps, band_freq, filter_first, filter_bias, filter_out, decay, out_weight
):
    rows, width = tokens.shape
    slab = in_weight.shape[2]
    channels = slab // n_seq
    per = rows // RADIX
    points = per * n_seq
    tables = dft_tables(points)
    anyspec = pl.BlockSpec(memory_space=pl.ANY)
    vspec = pl.BlockSpec(memory_space=pltpu.VMEM)
    dma = pltpu.SemaphoreType.DMA
    scratch = [
        pltpu.VMEM((rows, width), BF),
        pltpu.VMEM((3, width, slab), BF),
        *[pltpu.VMEM(t.shape, t.dtype) for t in tables],
        pltpu.VMEM((3, rows + 16, slab), F32),
        pltpu.VMEM((rows, slab), F32),
        pltpu.VMEM((3, 16, slab), BF),
        pltpu.VMEM((3, 16, slab), BF),
        pltpu.VMEM((per, slab, RADIX), BF),
        pltpu.VMEM((per, slab, RADIX), BF),
        pltpu.VMEM((points, channels, RADIX), BF),
        pltpu.VMEM((points, channels, RADIX), BF),
        pltpu.VMEM((points, channels, RADIX), BF),
        pltpu.VMEM((per, slab, RADIX), BF),
        pltpu.VMEM((points * channels, RADIX), F32),
        pltpu.VMEM((points, channels * RADIX), BF),
        pltpu.VMEM((2 * HALF, channels * RADIX), F32),
        pltpu.VMEM((channels * HALF, 2 * RADIX), BF),
        pltpu.VMEM((channels * HALF, 2 * RADIX), F32),
        pltpu.VMEM((channels * HALF, 2 * RADIX), F32),
        dma((10,)), dma((2, 3)), dma((n_seq,)), dma((n_seq,)), dma((n_seq,)), dma((n_seq,)), dma((n_seq,)), dma((n_seq,)),
        *spread_scratch(n_ch, rows, slab, out_weight.shape[1] // n_ch, per),
    ]
    return pl.pallas_call(
        functools.partial(operator_kernel, n_seq, n_ch),
        out_shape=jax.ShapeDtypeStruct((rows, slab), BF),
        in_specs=[anyspec] * 2 + [vspec] * 6 + [anyspec] * 6,
        out_specs=vspec,
        scratch_shapes=scratch,
        compiler_params=pltpu.CompilerParams(collective_id=0, has_side_effects=True, vmem_limit_bytes=56 * 2**20),
        cost_estimate=pl.CostEstimate(flops=2 * rows * width * slab * 3, bytes_accessed=12 * 2**20, transcendentals=0),
    )(
        tokens, jnp.transpose(in_weight, (1, 0, 2)), short_taps, band_freq[None, :], filter_first, filter_bias[None, :],
        filter_out, decay[None, :], *tables, out_weight,
    )


def local(tokens, in_weight, short_taps, band_freq, filter_first, filter_bias, filter_out, decay, out_weight):
    return operator_rows(
        lax.axis_size("seq"), lax.axis_size("ch"), tokens, in_weight, short_taps, band_freq, filter_first, filter_bias,
        filter_out, decay, out_weight,
    )


def solution(mesh):
    in_specs = (
        P("seq", None),
        P(None, None, "ch"),
        P(None, None, "ch"),
        P(),
        P(),
        P(),
        P(None, "ch"),
        P("ch"),
        P("ch", None),
    )
    out_specs = P("seq", "ch")
    return jax.shard_map(local, mesh=mesh, in_specs=in_specs, out_specs=out_specs, check_vma=False)
```

```python
import functools
import math

import jax
import jax.numpy as jnp
import numpy as np
from jax import lax
from jax.experimental import pallas as pl
from jax.experimental.pallas import tpu as pltpu
from jax.sharding import PartitionSpec as P

MESH = pl.DeviceIdType.MESH
BF = jnp.bfloat16
F32 = jnp.float32
HIGH = lax.Precision.HIGHEST
RADIX = 128
HALF = 80


def dft_tables(rows_in):
    full = RADIX * RADIX
    k1 = np.arange(HALF)[:, None]
    used = (k1 <= RADIX // 2).astype(np.float64)
    line = np.arange(RADIX)
    a = 2 * np.pi * k1 * np.arange(rows_in)[None, :] / RADIX
    outer = np.concatenate([np.cos(a) * used, -np.sin(a) * used], 0)
    tw = 2 * np.pi * k1 * line[None, :] / full
    twist = np.stack([np.cos(tw), np.sin(tw)])
    b = 2 * np.pi * np.outer(line, line) / RADIX
    co, si = np.cos(b), np.sin(b)
    inner = np.block([[co, -si], [si, co]])
    inner_back = np.block([[co, si], [-si, co]])
    weight = np.where((k1 == 0) | (k1 == RADIX // 2), 1.0, 2.0) * used / full
    outer_back = np.concatenate([(np.cos(a) * weight).T, (-np.sin(a) * weight).T], 1)
    return (
        jnp.asarray(outer, BF),
        jnp.asarray(twist, F32),
        jnp.asarray(inner, BF),
        jnp.asarray(inner_back, BF),
        jnp.asarray(outer_back, BF),
    )


def sin_turns(turns):
    turns = turns - 0.25
    turns = turns - jnp.round(turns)
    x = (0.25 - jnp.abs(turns)) * (2.0 * math.pi)
    x2 = x * x
    p = jnp.float32(-2.50521083854e-8)
    for c in (2.75573192239858e-6, -1.98412698412698e-4, 8.33333333333333e-3, -1.66666666666667e-1):
        p = p * x2 + jnp.float32(c)
    return x + x * x2 * p


def first_row(v):
    row = lax.broadcasted_iota(jnp.int32, (8, v.shape[1]), 0)
    return jnp.where(row == 0, jnp.broadcast_to(v, (8, v.shape[1])), 0.0)


def contract_rows(a, b):
    return lax.dot_general(a, b, (((0,), (0,)), ((), ())), precision=HIGH, preferred_element_type=F32)


def outer_product(v, w):
    return contract_rows(first_row(v), first_row(w))


def forward(grid32, x_all, a_all, rows_all, outer, twist, inner, spec_ref, channels):
    rows_in = x_all.shape[0]
    for c in range(channels):
        x_all[:, c * RADIX : (c + 1) * RADIX] = grid32[pl.ds(c, rows_in, stride=channels), :].astype(BF)
    a_all[...] = jnp.dot(outer[...], x_all[...], preferred_element_type=F32)
    co, si = twist[0], twist[1]
    for c in range(channels):
        lanes = slice(c * RADIX, (c + 1) * RADIX)
        re, im = a_all[:HALF, lanes], a_all[HALF:, lanes]
        rows = slice(c * HALF, (c + 1) * HALF)
        rows_all[rows, :RADIX] = (re * co + im * si).astype(BF)
        rows_all[rows, RADIX:] = (im * co - re * si).astype(BF)
    spec_ref[...] = jnp.dot(rows_all[...], inner[...], preferred_element_type=F32)


CHUNK = 64


class Spread:
    def __init__(self, n_ch, w_hbm, out_ref, wout, g2, sums, landed, wl_sem, wx_ssem, wx_rsem, wc_ssem, wc_rsem, r_ssem, r_rsem):
        self.__dict__.update(locals())
        del self.__dict__["self"]
        self.n_z = n_ch // 2
        self.c = lax.axis_index("ch")
        self.z = self.c // 2
        self.xl = lax.rem(self.c, 2)
        self.s = lax.axis_index("seq")
        self.core = lax.rem(self.s, 2)
        self.across = self.c + 1 - 2 * self.xl
        far = lax.rem(self.s // 2, 2)
        self.sides = [(self.s, self.across), (self.s + 2 - 4 * far, self.across)]
        self.sibling = {"seq": self.s + 1 - 2 * self.core}
        self.up = {"ch": lax.rem(self.c + 2, n_ch)}
        self.down = {"ch": lax.rem(self.c + n_ch - 2, n_ch)}
        self.depth = w_hbm.shape[0]
        self.cols = w_hbm.shape[1] // n_ch
        self.rows = out_ref.shape[0]
        self.chunks = self.rows // CHUNK
        half = self.n_z // 2
        shifts = [half] + [x for k in range(half - 1, 0, -1) for x in (k, self.n_z - k)] + [0]
        self.need = [lax.rem(self.z + k, self.n_z) for k in shifts]

    def _columns(self, block):
        return pl.ds(pl.multiple_of(block * self.cols, self.cols), self.cols)

    def own_weight(self, j):
        return pltpu.make_async_copy(
            self.w_hbm.at[:, self._columns(2 * j + self.xl)], self.wout.at[0, j], self.wl_sem.at[j]
        )

    def weight_to_side(self, k, side):
        j = self.need[k]
        part = self.depth // 4
        line = pl.ds(pl.multiple_of(self.core * 2 * part + side * part, part), part)
        return pltpu.make_async_remote_copy(
            src_ref=self.w_hbm.at[line, self._columns(2 * j + 1 - self.xl)],
            dst_ref=self.wout.at[1, j, line, :],
            send_sem=self.wx_ssem.at[side, k], recv_sem=self.wx_rsem.at[side, k],
            device_id=self.sides[side], device_id_type=MESH,
        )

    def weight_to_sibling(self, k, core):
        half = self.depth // 2
        piece = self.wout.at[1, self.need[k], pl.ds(pl.multiple_of(core * half, half), half), :]
        return pltpu.make_async_remote_copy(
            src_ref=piece, dst_ref=piece, send_sem=self.wc_ssem.at[k], recv_sem=self.wc_rsem.at[k],
            device_id=self.sibling, device_id_type=MESH,
        )

    def start_weights(self, blocks):
        for k in blocks:
            for side in (0, 1):
                self.weight_to_side(k, side).start()

    def load_weights(self):
        for j in range(self.n_z):
            self.own_weight(j).start()

    def pass_weights(self, blocks):
        for k in blocks:
            for side in (0, 1):
                self.weight_to_side(k, side).wait()
            self.weight_to_sibling(k, self.core).start()

    def take_weights(self, blocks):
        for k in blocks:
            self.weight_to_sibling(k, self.core).wait_send()
            self.weight_to_sibling(k, 1 - self.core).wait_recv()

    def hop(self, way, step, i):
        return pltpu.make_async_remote_copy(
            src_ref=self.sums.at[way, step, i], dst_ref=self.landed.at[way, step, i],
            send_sem=self.r_ssem.at[way, step, i], recv_sem=self.r_rsem.at[way, step, i],
            device_id=(self.up, self.down)[way], device_id_type=MESH,
        )

    def partial_sum(self, block, i):
        line = pl.ds(pl.multiple_of(i * CHUNK, CHUNK), CHUNK)
        return jnp.dot(self.g2[0, line], self.wout[0, block], preferred_element_type=F32) + jnp.dot(
            self.g2[1, line], self.wout[1, block], preferred_element_type=F32
        )

    def block_at(self, way, step):
        n = self.n_z
        if way == 0:
            return lax.rem(self.z + n // 2 - step, n)
        return lax.rem(self.z + n // 2 + step, n)

    def send(self, way, step, i, fresh):
        own = self.partial_sum(self.block_at(way, step), i)
        if not fresh:
            self.hop(way, step - 1, i).wait_recv()
            own = own + self.landed[way, step - 1, i].astype(F32)
        self.sums[way, step, i] = own.astype(BF)
        self.hop(way, step, i).start()

    def finish(self):
        for j in range(self.n_z):
            self.own_weight(j).wait()
        half = self.chunks // 2

        def both(step, first, fresh):
            def body(i, carry):
                self.send(0, step, i if first else half + i, fresh)
                self.send(1, step, half + i if first else i, fresh)
                return carry

            lax.fori_loop(0, half, body, 0)

        self.take_weights([0])
        both(0, True, True)
        self.take_weights([1, 2])
        both(1, False, True)
        self.pass_weights(range(3, self.n_z))
        both(1, True, False)
        steps = self.n_z // 2
        for step in range(2, steps):
            self.take_weights([2 * step - 1, 2 * step])
            both(step, False, False)
            both(step, True, False)
        self.take_weights([self.n_z - 1])

        def home(i, carry):
            own = self.partial_sum(self.z, i)
            self.hop(0, steps - 1, i).wait_recv()
            self.hop(1, steps - 1, i).wait_recv()
            own = own + self.landed[0, steps - 1, i].astype(F32) + self.landed[1, steps - 1, i].astype(F32)
            self.out_ref[pl.ds(pl.multiple_of(i * CHUNK, CHUNK), CHUNK), :] = own.astype(BF)
            return carry

        lax.fori_loop(0, self.chunks, home, 0)

        def drain(i, carry):
            for step in range(1, steps):
                self.hop(0, step, i).wait_send()
                self.hop(1, step, i).wait_send()
            return carry

        lax.fori_loop(0, self.chunks, drain, 0)

        def drain_first(i, carry):
            self.hop(0, 0, i).wait_send()
            self.hop(1, 0, half + i).wait_send()
            return carry

        lax.fori_loop(0, half, drain_first, 0)


def spread_scratch(n_ch, rows, depth, cols):
    n_z = n_ch // 2
    dma = pltpu.SemaphoreType.DMA
    return [
        pltpu.VMEM((2, n_z, depth, cols), BF),
        pltpu.VMEM((2, rows, depth), BF),
        pltpu.VMEM((2, n_z // 2, rows // CHUNK, CHUNK, cols), BF),
        pltpu.VMEM((2, n_z // 2, rows // CHUNK, CHUNK, cols), BF),
        dma((n_z,)), dma((2, n_z)), dma((2, n_z)), dma((n_z,)), dma((n_z,)),
        dma((2, n_z // 2, rows // CHUNK)), dma((2, n_z // 2, rows // CHUNK)),
    ]


def operator_kernel(
    n_seq, n_ch,
    tok_hbm, w_hbm, taps, band, first, bias, fout, decay, outer_hbm, twist_hbm, inner_hbm, inner_back_hbm, outer_back_hbm, wout_hbm,
    out_ref,
    tok, w, outer, twist, inner, inner_back, outer_back,
    tap_cols, padded, send4, imp4, imp_recv, pro_recv, gated_send, gated,
    grid32, x_all, a_all, rows_all, imp_spec, src_spec,
    load_sem, imp_ssem, imp_rsem, pro_ssem, pro_rsem, gat_ssem, gat_rsem, *out_scratch,
):
    me = lax.axis_index("seq")
    out = Spread(n_ch, wout_hbm, out_ref, *out_scratch)
    rows, width = tok_hbm.shape
    slab = w_hbm.shape[2]
    channels = slab // n_seq
    per = rows // RADIX
    points = per * n_seq
    half = rows // 2
    length = rows * n_seq

    loads = [
        pltpu.make_async_copy(w_hbm.at[0], w.at[0], load_sem.at[0]),
        pltpu.make_async_copy(tok_hbm.at[:half], tok.at[:half], load_sem.at[1]),
        pltpu.make_async_copy(tok_hbm.at[half:], tok.at[half:], load_sem.at[2]),
        pltpu.make_async_copy(w_hbm.at[2], w.at[2], load_sem.at[3]),
        pltpu.make_async_copy(w_hbm.at[1], w.at[1], load_sem.at[4]),
        pltpu.make_async_copy(outer_hbm, outer, load_sem.at[5]),
        pltpu.make_async_copy(twist_hbm, twist, load_sem.at[6]),
        pltpu.make_async_copy(inner_hbm, inner, load_sem.at[7]),
        pltpu.make_async_copy(inner_back_hbm, inner_back, load_sem.at[8]),
        pltpu.make_async_copy(outer_back_hbm, outer_back, load_sem.at[9]),
    ]
    for copy in loads:
        copy.start()
    out.load_weights()

    barrier = pltpu.get_barrier_semaphore()

    def greet(d, carry):
        pl.semaphore_signal(barrier, inc=1, device_id={"seq": lax.rem(me + d, n_seq)}, device_id_type=MESH)
        return carry

    lax.fori_loop(1, n_seq, greet, 0)

    def greet_across(p, carry):
        pl.semaphore_signal(barrier, inc=1, device_id=(p, out.across), device_id_type=MESH)
        return carry

    lax.fori_loop(0, n_seq, greet_across, 0)
    for peer in (out.up, out.down):
        pl.semaphore_signal(barrier, inc=1, device_id=peer, device_id_type=MESH)

    pos = (me * rows + lax.broadcasted_iota(jnp.int32, (1, rows), 1)).astype(F32)
    scaled = pos * (1.0 / length)
    turns = outer_product(band[...], scaled)
    turns = turns - jnp.round(turns)
    n_band = band.shape[1]
    head = lax.broadcasted_iota(jnp.int32, (8, rows), 0)
    features = jnp.concatenate(
        [sin_turns(turns + 0.25), sin_turns(turns), jnp.where(head == 0, scaled, jnp.where(head == 1, 1.0, 0.0))], 0
    )
    head = lax.broadcasted_iota(jnp.int32, (8, first.shape[1]), 0)
    layer = jnp.concatenate(
        [
            first[1 : 1 + n_band, :],
            first[1 + n_band :, :],
            jnp.where(head == 0, first[0:1, :], jnp.where(head == 1, bias[...], 0.0)),
        ],
        0,
    )
    pre = contract_rows(layer, features)
    hidden = sin_turns(pre * (1.0 / (2.0 * math.pi)))
    impulse = contract_rows(fout[...], hidden) * jnp.exp(-outer_product(decay[...], pos))
    for q in range(per):
        imp4[q] = impulse[:, q * RADIX : (q + 1) * RADIX].astype(BF)

    for g in range(3):
        for i in range(3):
            tap_cols[g, i] = jnp.broadcast_to(taps[i, g : g + 1, :], (RADIX, slab)).T
        padded[g, 0:channels, :] = jnp.zeros((channels, RADIX), F32)

    mine = pl.ds(pl.multiple_of(me * channels, channels), channels)

    def spread_copy(src, dst, ssem, rsem, peer):
        return pltpu.make_async_remote_copy(
            src_ref=src.at[:, pl.ds(pl.multiple_of(peer * channels, channels), channels), :],
            dst_ref=dst.at[pl.ds(me * per, per)],
            send_sem=ssem.at[peer],
            recv_sem=rsem.at[me],
            device_id={"seq": peer},
            device_id_type=MESH,
        )

    def arrive(dst, ssem, rsem, peer):
        piece = dst.at[pl.ds(peer * per, per)]
        return pltpu.make_async_remote_copy(
            src_ref=piece, dst_ref=piece, send_sem=ssem.at[peer], recv_sem=rsem.at[peer],
            device_id={"seq": peer}, device_id_type=MESH,
        )

    def own_piece(src, dst):
        dst[pl.ds(me * per, per)] = src[:, mine, :]

    def each_peer(step):
        def body(d, carry):
            step(lax.rem(me + d, n_seq))
            return carry

        lax.fori_loop(1, n_seq, body, 0)

    def project(g):
        for part in (0, 1):
            if g == 0:
                loads[1 + part].wait()
            y = jnp.dot(tok[part * half : (part + 1) * half, :], w[g], preferred_element_type=F32)
            for q in range(per // 2):
                send4[g, part * (per // 2) + q] = y[q * RADIX : (q + 1) * RADIX, :].T.astype(BF)

    def project_copy(g, p):
        return spread_copy(send4.at[g], pro_recv.at[g], pro_ssem.at[g], pro_rsem.at[g], p)

    def mixed(g, row, count):
        lane = lax.broadcasted_iota(jnp.int32, (count, RADIX), 1)
        now = padded[g, pl.ds(channels + row, count), :]
        before = padded[g, pl.ds(row, count), :]
        total = jnp.zeros((count // channels, channels, RADIX), F32)
        for i in range(3):
            moved = now if i == 0 else pltpu.roll(jnp.where(lane >= RADIX - i, before, now), i, 1)
            total = total + tap_cols[g, i, mine, :][None] * moved.reshape(count // channels, channels, RADIX)
        return total.reshape(count, RADIX)

    def take_projected(g):
        each_peer(lambda p: arrive(pro_recv.at[g], pro_ssem.at[g], pro_rsem.at[g], p).wait_recv())
        padded[g, channels:, :] = pro_recv[g].astype(F32).reshape(points * channels, RADIX)

    block = 8 * channels

    def each_block(step):
        def body(i, carry):
            step(pl.multiple_of(i * block, block))
            return carry

        lax.fori_loop(0, points * channels // block, body, 0)

    loads[0].wait()
    project(0)
    pl.semaphore_wait(barrier, 2 * n_seq + 1)
    each_peer(lambda p: project_copy(0, p).start())
    loads[3].wait()
    project(2)
    each_peer(lambda p: project_copy(2, p).start())
    each_peer(lambda p: spread_copy(imp4, imp_recv, imp_ssem, imp_rsem, p).start())
    out.start_weights(range(3))
    loads[4].wait()
    project(1)
    each_peer(lambda p: project_copy(1, p).start())
    out.start_weights(range(3, out.n_z))
    own_piece(imp4, imp_recv)
    for g in range(3):
        own_piece(send4.at[g], pro_recv.at[g])
    for copy in loads[5:]:
        copy.wait()

    each_peer(lambda p: arrive(imp_recv, imp_ssem, imp_rsem, p).wait_recv())
    grid32[...] = imp_recv[...].astype(F32).reshape(points * channels, RADIX)
    forward(grid32, x_all, a_all, rows_all, outer, twist, inner, imp_spec, channels)

    take_projected(0)
    take_projected(2)

    def source_block(row):
        grid32[pl.ds(row, block), :] = mixed(0, row, block) * mixed(2, row, block)

    each_block(source_block)
    forward(grid32, x_all, a_all, rows_all, outer, twist, inner, src_spec, channels)

    for c in range(channels):
        line = slice(c * HALF, (c + 1) * HALF)
        sre, sim = src_spec[line, :RADIX], src_spec[line, RADIX:]
        ire, iim = imp_spec[line, :RADIX], imp_spec[line, RADIX:]
        rows_all[line, :RADIX] = (sre * ire - sim * iim).astype(BF)
        rows_all[line, RADIX:] = (sre * iim + sim * ire).astype(BF)
    src_spec[...] = jnp.dot(rows_all[...], inner_back[...], preferred_element_type=F32)
    co, si = twist[0], twist[1]
    for c in range(channels):
        line = slice(c * HALF, (c + 1) * HALF)
        lanes = slice(c * RADIX, (c + 1) * RADIX)
        re, im = src_spec[line, :RADIX], src_spec[line, RADIX:]
        back = jnp.concatenate([re * co - im * si, im * co + re * si], 0).astype(BF)
        y = jnp.dot(outer_back[...], back, preferred_element_type=F32)
        grid32[pl.ds(c, points, stride=channels), :] = y
    take_projected(1)

    def gate_block(row):
        value = grid32[pl.ds(row, block), :] * mixed(1, row, block)
        gated_send[pl.ds(row // channels, 8)] = value.astype(BF).reshape(8, channels, RADIX)

    each_block(gate_block)

    def gated_copy(side, peer):
        return pltpu.make_async_remote_copy(
            src_ref=gated_send.at[pl.ds(peer * per, per)],
            dst_ref=gated.at[side, :, mine, :],
            send_sem=gat_ssem.at[side, peer],
            recv_sem=gat_rsem.at[side, me],
            device_id=(peer, out.across if side else out.c),
            device_id_type=MESH,
        )

    def gated_arrive(side, peer):
        piece = gated.at[side, :, pl.ds(pl.multiple_of(peer * channels, channels), channels), :]
        return pltpu.make_async_remote_copy(
            src_ref=piece, dst_ref=piece, send_sem=gat_ssem.at[side, peer], recv_sem=gat_rsem.at[side, peer],
            device_id=(peer, out.across if side else out.c), device_id_type=MESH,
        )

    def both_sides(p):
        gated_copy(0, p).start()
        gated_copy(1, p).start()

    each_peer(both_sides)
    gated_copy(1, me).start()
    gated[0, :, mine, :] = gated_send[pl.ds(me * per, per)]
    out.pass_weights(range(3))
    for side in (0, 1):
        each_peer(lambda p: gated_arrive(side, p).wait_recv())
        if side:
            gated_arrive(1, me).wait_recv()
        for q in range(per):
            out.g2[side, q * RADIX : (q + 1) * RADIX, :] = gated[side, q].astype(F32).T.astype(BF)
    out.finish()

    each_peer(lambda p: spread_copy(imp4, imp_recv, imp_ssem, imp_rsem, p).wait_send())
    for g in range(3):
        each_peer(lambda p: project_copy(g, p).wait_send())
    for side in (0, 1):
        each_peer(lambda p: gated_copy(side, p).wait_send())
    gated_copy(1, me).wait_send()


def operator_rows(
    n_seq, n_ch, tokens, in_weight, short_taps, band_freq, filter_first, filter_bias, filter_out, decay, out_weight
):
    rows, width = tokens.shape
    slab = in_weight.shape[2]
    channels = slab // n_seq
    per = rows // RADIX
    points = per * n_seq
    tables = dft_tables(points)
    anyspec = pl.BlockSpec(memory_space=pl.ANY)
    vspec = pl.BlockSpec(memory_space=pltpu.VMEM)
    dma = pltpu.SemaphoreType.DMA
    scratch = [
        pltpu.VMEM((rows, width), BF),
        pltpu.VMEM((3, width, slab), BF),
        *[pltpu.VMEM(t.shape, t.dtype) for t in tables],
        pltpu.VMEM((3, 3, slab, RADIX), F32),
        pltpu.VMEM((3, (points + 1) * channels, RADIX), F32),
        pltpu.VMEM((3, per, slab, RADIX), BF),
        pltpu.VMEM((per, slab, RADIX), BF),
        pltpu.VMEM((points, channels, RADIX), BF),
        pltpu.VMEM((3, points, channels, RADIX), BF),
        pltpu.VMEM((points, channels, RADIX), BF),
        pltpu.VMEM((2, per, slab, RADIX), BF),
        pltpu.VMEM((points * channels, RADIX), F32),
        pltpu.VMEM((points, channels * RADIX), BF),
        pltpu.VMEM((2 * HALF, channels * RADIX), F32),
        pltpu.VMEM((channels * HALF, 2 * RADIX), BF),
        pltpu.VMEM((channels * HALF, 2 * RADIX), F32),
        pltpu.VMEM((channels * HALF, 2 * RADIX), F32),
        dma((10,)), dma((n_seq,)), dma((n_seq,)), dma((3, n_seq)), dma((3, n_seq)), dma((2, n_seq)), dma((2, n_seq)),
        *spread_scratch(n_ch, rows, slab, out_weight.shape[1] // n_ch),
    ]
    return pl.pallas_call(
        functools.partial(operator_kernel, n_seq, n_ch),
        out_shape=jax.ShapeDtypeStruct((rows, slab), BF),
        in_specs=[anyspec] * 2 + [vspec] * 6 + [anyspec] * 6,
        out_specs=vspec,
        scratch_shapes=scratch,
        compiler_params=pltpu.CompilerParams(collective_id=0, has_side_effects=True, vmem_limit_bytes=56 * 2**20),
        cost_estimate=pl.CostEstimate(flops=2 * rows * width * slab * 3, bytes_accessed=12 * 2**20, transcendentals=0),
    )(
        tokens, jnp.transpose(in_weight, (1, 0, 2)), short_taps, band_freq[None, :], filter_first, filter_bias[None, :],
        filter_out, decay[None, :], *tables, out_weight,
    )


def local(tokens, in_weight, short_taps, band_freq, filter_first, filter_bias, filter_out, decay, out_weight):
    return operator_rows(
        lax.axis_size("seq"), lax.axis_size("ch"), tokens, in_weight, short_taps, band_freq, filter_first, filter_bias,
        filter_out, decay, out_weight,
    )


def solution(mesh):
    in_specs = (
        P("seq", None),
        P(None, None, "ch"),
        P(None, None, "ch"),
        P(),
        P(),
        P(),
        P(None, "ch"),
        P("ch"),
        P("ch", None),
    )
    out_specs = P("seq", "ch")
    return jax.shard_map(local, mesh=mesh, in_specs=in_specs, out_specs=out_specs, check_vma=False)
```

```python
import functools
import math

import jax
import jax.numpy as jnp
import numpy as np
from jax import lax
from jax.experimental import pallas as pl
from jax.experimental.pallas import tpu as pltpu
from jax.sharding import PartitionSpec as P

MESH = pl.DeviceIdType.MESH
BF = jnp.bfloat16
F32 = jnp.float32
HIGH = lax.Precision.HIGHEST
RADIX = 128
HALF = 80


def dft_tables(rows_in):
    full = RADIX * RADIX
    k1 = np.arange(HALF)[:, None]
    used = (k1 <= RADIX // 2).astype(np.float64)
    line = np.arange(RADIX)
    a = 2 * np.pi * k1 * np.arange(rows_in)[None, :] / RADIX
    outer = np.concatenate([np.cos(a) * used, -np.sin(a) * used], 0)
    tw = 2 * np.pi * k1 * line[None, :] / full
    twist = np.stack([np.cos(tw), np.sin(tw)])
    b = 2 * np.pi * np.outer(line, line) / RADIX
    co, si = np.cos(b), np.sin(b)
    inner = np.block([[co, -si], [si, co]])
    inner_back = np.block([[co, si], [-si, co]])
    weight = np.where((k1 == 0) | (k1 == RADIX // 2), 1.0, 2.0) * used / full
    outer_back = np.concatenate([(np.cos(a) * weight).T, (-np.sin(a) * weight).T], 1)
    return (
        jnp.asarray(outer, BF),
        jnp.asarray(twist, F32),
        jnp.asarray(inner, BF),
        jnp.asarray(inner_back, BF),
        jnp.asarray(outer_back, BF),
    )


def sin_turns(turns):
    turns = turns - 0.25
    turns = turns - jnp.round(turns)
    x = (0.25 - jnp.abs(turns)) * (2.0 * math.pi)
    x2 = x * x
    p = jnp.float32(-2.50521083854e-8)
    for c in (2.75573192239858e-6, -1.98412698412698e-4, 8.33333333333333e-3, -1.66666666666667e-1):
        p = p * x2 + jnp.float32(c)
    return x + x * x2 * p


def first_row(v):
    row = lax.broadcasted_iota(jnp.int32, (8, v.shape[1]), 0)
    return jnp.where(row == 0, jnp.broadcast_to(v, (8, v.shape[1])), 0.0)


def contract_rows(a, b):
    return lax.dot_general(a, b, (((0,), (0,)), ((), ())), precision=HIGH, preferred_element_type=F32)


def outer_product(v, w):
    return contract_rows(first_row(v), first_row(w))


def forward(grid32, x_all, a_all, rows_all, outer, twist, inner, spec_ref, channels):
    rows_in = x_all.shape[0]
    for c in range(channels):
        x_all[:, c * RADIX : (c + 1) * RADIX] = grid32[pl.ds(c, rows_in, stride=channels), :].astype(BF)
    a_all[...] = jnp.dot(outer[...], x_all[...], preferred_element_type=F32)
    co, si = twist[0], twist[1]
    for c in range(channels):
        lanes = slice(c * RADIX, (c + 1) * RADIX)
        re, im = a_all[:HALF, lanes], a_all[HALF:, lanes]
        rows = slice(c * HALF, (c + 1) * HALF)
        rows_all[rows, :RADIX] = (re * co + im * si).astype(BF)
        rows_all[rows, RADIX:] = (im * co - re * si).astype(BF)
    spec_ref[...] = jnp.dot(rows_all[...], inner[...], preferred_element_type=F32)


CHUNK = 64


class Spread:
    def __init__(self, n_ch, w_hbm, out_ref, wout, g2, sums, landed, wl_sem, wx_ssem, wx_rsem, wc_ssem, wc_rsem, r_ssem, r_rsem):
        self.__dict__.update(locals())
        del self.__dict__["self"]
        self.n_z = n_ch // 2
        self.c = lax.axis_index("ch")
        self.z = self.c // 2
        self.xl = lax.rem(self.c, 2)
        self.s = lax.axis_index("seq")
        self.core = lax.rem(self.s, 2)
        self.across = self.c + 1 - 2 * self.xl
        far = lax.rem(self.s // 2, 2)
        self.sides = [(self.s, self.across), (self.s + 2 - 4 * far, self.across)]
        self.sibling = {"seq": self.s + 1 - 2 * self.core}
        self.up = {"ch": lax.rem(self.c + 2, n_ch)}
        self.down = {"ch": lax.rem(self.c + n_ch - 2, n_ch)}
        self.depth = w_hbm.shape[0]
        self.cols = w_hbm.shape[1] // n_ch
        self.rows = out_ref.shape[0]
        self.chunks = self.rows // CHUNK
        half = self.n_z // 2
        shifts = [half] + [x for k in range(half - 1, 0, -1) for x in (k, self.n_z - k)] + [0]
        self.need = [lax.rem(self.z + k, self.n_z) for k in shifts]

    def _columns(self, block):
        return pl.ds(pl.multiple_of(block * self.cols, self.cols), self.cols)

    def own_weight(self, j):
        return pltpu.make_async_copy(
            self.w_hbm.at[:, self._columns(2 * j + self.xl)], self.wout.at[0, j], self.wl_sem.at[j]
        )

    def weight_to_side(self, k, side):
        j = self.need[k]
        part = self.depth // 4
        line = pl.ds(pl.multiple_of(self.core * 2 * part + side * part, part), part)
        return pltpu.make_async_remote_copy(
            src_ref=self.w_hbm.at[line, self._columns(2 * j + 1 - self.xl)],
            dst_ref=self.wout.at[1, j, line, :],
            send_sem=self.wx_ssem.at[side, k], recv_sem=self.wx_rsem.at[side, k],
            device_id=self.sides[side], device_id_type=MESH,
        )

    def weight_to_sibling(self, k, core):
        half = self.depth // 2
        piece = self.wout.at[1, self.need[k], pl.ds(pl.multiple_of(core * half, half), half), :]
        return pltpu.make_async_remote_copy(
            src_ref=piece, dst_ref=piece, send_sem=self.wc_ssem.at[k], recv_sem=self.wc_rsem.at[k],
            device_id=self.sibling, device_id_type=MESH,
        )

    def start_weights(self, blocks):
        for k in blocks:
            for side in (0, 1):
                self.weight_to_side(k, side).start()

    def load_weights(self):
        for j in range(self.n_z):
            self.own_weight(j).start()

    def pass_weights(self, blocks):
        for k in blocks:
            for side in (0, 1):
                self.weight_to_side(k, side).wait()
            self.weight_to_sibling(k, self.core).start()

    def take_weights(self, blocks):
        for k in blocks:
            self.weight_to_sibling(k, self.core).wait_send()
            self.weight_to_sibling(k, 1 - self.core).wait_recv()

    def hop(self, way, step, i):
        return pltpu.make_async_remote_copy(
            src_ref=self.sums.at[way, step, i], dst_ref=self.landed.at[way, step, i],
            send_sem=self.r_ssem.at[way, step, i], recv_sem=self.r_rsem.at[way, step, i],
            device_id=(self.up, self.down)[way], device_id_type=MESH,
        )

    def partial_sum(self, block, i):
        line = pl.ds(pl.multiple_of(i * CHUNK, CHUNK), CHUNK)
        return jnp.dot(self.g2[0, line], self.wout[0, block], preferred_element_type=F32) + jnp.dot(
            self.g2[1, line], self.wout[1, block], preferred_element_type=F32
        )

    def block_at(self, way, step):
        n = self.n_z
        if way == 0:
            return lax.rem(self.z + n // 2 - step, n)
        return lax.rem(self.z + n // 2 + step, n)

    def send(self, way, step, i, fresh):
        own = self.partial_sum(self.block_at(way, step), i)
        if not fresh:
            self.hop(way, step - 1, i).wait_recv()
            own = own + self.landed[way, step - 1, i].astype(F32)
        self.sums[way, step, i] = own.astype(BF)
        self.hop(way, step, i).start()

    def finish(self, take_gated):
        for j in range(self.n_z):
            self.own_weight(j).wait()
        half = self.chunks // 2

        def both(steps, firsts, fresh):
            def body(i, carry):
                for way in (0, 1):
                    self.send(way, steps[way], i if firsts[way] else half + i, fresh)
                return carry

            lax.fori_loop(0, half, body, 0)

        self.take_weights([0, 1, 2])
        take_gated(0)
        both((0, 1), (True, True), True)
        take_gated(1)
        both((1, 0), (False, False), True)
        self.pass_weights(range(3, self.n_z))
        both((1, 1), (True, False), False)
        steps = self.n_z // 2
        for step in range(2, steps):
            self.take_weights([2 * step - 1, 2 * step])
            both((step, step), (False, True), False)
            both((step, step), (True, False), False)
        self.take_weights([self.n_z - 1])

        def home(i, carry):
            own = self.partial_sum(self.z, i)
            self.hop(0, steps - 1, i).wait_recv()
            self.hop(1, steps - 1, i).wait_recv()
            own = own + self.landed[0, steps - 1, i].astype(F32) + self.landed[1, steps - 1, i].astype(F32)
            self.out_ref[pl.ds(pl.multiple_of(i * CHUNK, CHUNK), CHUNK), :] = own.astype(BF)
            return carry

        lax.fori_loop(0, self.chunks, home, 0)

        def drain(i, carry):
            for step in range(1, steps):
                self.hop(0, step, i).wait_send()
                self.hop(1, step, i).wait_send()
            return carry

        lax.fori_loop(0, self.chunks, drain, 0)

        def drain_first(i, carry):
            self.hop(0, 0, i).wait_send()
            self.hop(1, 0, half + i).wait_send()
            return carry

        lax.fori_loop(0, half, drain_first, 0)


def spread_scratch(n_ch, rows, depth, cols):
    n_z = n_ch // 2
    dma = pltpu.SemaphoreType.DMA
    return [
        pltpu.VMEM((2, n_z, depth, cols), BF),
        pltpu.VMEM((2, rows, depth), BF),
        pltpu.VMEM((2, n_z // 2, rows // CHUNK, CHUNK, cols), BF),
        pltpu.VMEM((2, n_z // 2, rows // CHUNK, CHUNK, cols), BF),
        dma((n_z,)), dma((2, n_z)), dma((2, n_z)), dma((n_z,)), dma((n_z,)),
        dma((2, n_z // 2, rows // CHUNK)), dma((2, n_z // 2, rows // CHUNK)),
    ]


def operator_kernel(
    n_seq, n_ch,
    tok_hbm, w_hbm, taps, band, first, bias, fout, decay, outer_hbm, twist_hbm, inner_hbm, inner_back_hbm, outer_back_hbm, wout_hbm,
    out_ref,
    tok, w, outer, twist, inner, inner_back, outer_back,
    tap_cols, fout_rows, decay_cols, padded, send4, pro_recv, gated_send, gated,
    grid32, x_all, a_all, rows_all, imp_spec, src_spec,
    load_sem, pro_ssem, pro_rsem, gat_ssem, gat_rsem, *out_scratch,
):
    me = lax.axis_index("seq")
    out = Spread(n_ch, wout_hbm, out_ref, *out_scratch)
    rows, width = tok_hbm.shape
    slab = w_hbm.shape[2]
    channels = slab // n_seq
    per = rows // RADIX
    points = per * n_seq
    half = rows // 2
    length = rows * n_seq

    loads = [
        pltpu.make_async_copy(w_hbm.at[0], w.at[0], load_sem.at[0]),
        pltpu.make_async_copy(tok_hbm.at[:half], tok.at[:half], load_sem.at[1]),
        pltpu.make_async_copy(tok_hbm.at[half:], tok.at[half:], load_sem.at[2]),
        pltpu.make_async_copy(w_hbm.at[2], w.at[2], load_sem.at[3]),
        pltpu.make_async_copy(w_hbm.at[1], w.at[1], load_sem.at[4]),
        pltpu.make_async_copy(outer_hbm, outer, load_sem.at[5]),
        pltpu.make_async_copy(twist_hbm, twist, load_sem.at[6]),
        pltpu.make_async_copy(inner_hbm, inner, load_sem.at[7]),
        pltpu.make_async_copy(inner_back_hbm, inner_back, load_sem.at[8]),
        pltpu.make_async_copy(outer_back_hbm, outer_back, load_sem.at[9]),
    ]
    for copy in loads:
        copy.start()

    barrier = pltpu.get_barrier_semaphore()

    def greet(d, carry):
        pl.semaphore_signal(barrier, inc=1, device_id={"seq": lax.rem(me + d, n_seq)}, device_id_type=MESH)
        return carry

    lax.fori_loop(1, n_seq, greet, 0)

    def greet_across(p, carry):
        pl.semaphore_signal(barrier, inc=1, device_id=(p, out.across), device_id_type=MESH)
        return carry

    lax.fori_loop(0, n_seq, greet_across, 0)
    for peer in (out.up, out.down):
        pl.semaphore_signal(barrier, inc=1, device_id=peer, device_id_type=MESH)

    for g in range(3):
        for i in range(3):
            tap_cols[g, i] = jnp.broadcast_to(taps[i, g : g + 1, :], (RADIX, slab)).T
        padded[g, 0:channels, :] = jnp.zeros((channels, RADIX), F32)
    fout_rows[...] = fout[...].T
    decay_cols[...] = jnp.broadcast_to(decay[...], (RADIX, slab)).T

    mine = pl.ds(pl.multiple_of(me * channels, channels), channels)

    def spread_copy(src, dst, ssem, rsem, peer):
        return pltpu.make_async_remote_copy(
            src_ref=src.at[:, pl.ds(pl.multiple_of(peer * channels, channels), channels), :],
            dst_ref=dst.at[pl.ds(me * per, per)],
            send_sem=ssem.at[peer],
            recv_sem=rsem.at[me],
            device_id={"seq": peer},
            device_id_type=MESH,
        )

    def arrive(dst, ssem, rsem, peer):
        piece = dst.at[pl.ds(peer * per, per)]
        return pltpu.make_async_remote_copy(
            src_ref=piece, dst_ref=piece, send_sem=ssem.at[peer], recv_sem=rsem.at[peer],
            device_id={"seq": peer}, device_id_type=MESH,
        )

    def own_piece(src, dst):
        dst[pl.ds(me * per, per)] = src[:, mine, :]

    def each_peer(step):
        def body(d, carry):
            step(lax.rem(me + d, n_seq))
            return carry

        lax.fori_loop(1, n_seq, body, 0)

    def project(g):
        for part in (0, 1):
            if g == 0:
                loads[1 + part].wait()
            y = jnp.dot(tok[part * half : (part + 1) * half, :], w[g], preferred_element_type=F32)
            for q in range(per // 2):
                send4[g, part * (per // 2) + q] = y[q * RADIX : (q + 1) * RADIX, :].T.astype(BF)

    def project_copy(g, p):
        return spread_copy(send4.at[g], pro_recv.at[g], pro_ssem.at[g], pro_rsem.at[g], p)

    def mixed(g, row, count):
        lane = lax.broadcasted_iota(jnp.int32, (count, RADIX), 1)
        now = padded[g, pl.ds(channels + row, count), :]
        before = padded[g, pl.ds(row, count), :]
        total = jnp.zeros((count // channels, channels, RADIX), F32)
        for i in range(3):
            moved = now if i == 0 else pltpu.roll(jnp.where(lane >= RADIX - i, before, now), i, 1)
            total = total + tap_cols[g, i, mine, :][None] * moved.reshape(count // channels, channels, RADIX)
        return total.reshape(count, RADIX)

    def take_projected(g):
        each_peer(lambda p: arrive(pro_recv.at[g], pro_ssem.at[g], pro_rsem.at[g], p).wait_recv())
        padded[g, channels:, :] = pro_recv[g].astype(F32).reshape(points * channels, RADIX)

    block = 8 * channels

    def each_block(step):
        def body(i, carry):
            step(pl.multiple_of(i * block, block))
            return carry

        lax.fori_loop(0, points * channels // block, body, 0)

    n_band = band.shape[1]
    stretch = 2 * rows

    def filter_block(step, carry):
        pos = (step * stretch + lax.broadcasted_iota(jnp.int32, (1, stretch), 1)).astype(F32)
        scaled = pos * (1.0 / length)
        turns = outer_product(band[...], scaled)
        turns = turns - jnp.round(turns)
        head = lax.broadcasted_iota(jnp.int32, (8, stretch), 0)
        features = jnp.concatenate(
            [sin_turns(turns + 0.25), sin_turns(turns), jnp.where(head == 0, scaled, jnp.where(head == 1, 1.0, 0.0))], 0
        )
        head = lax.broadcasted_iota(jnp.int32, (8, first.shape[1]), 0)
        layer = jnp.concatenate(
            [
                first[1 : 1 + n_band, :],
                first[1 + n_band :, :],
                jnp.where(head == 0, first[0:1, :], jnp.where(head == 1, bias[...], 0.0)),
            ],
            0,
        )
        hidden = sin_turns(contract_rows(layer, features) * (1.0 / (2.0 * math.pi)))
        shaped = jnp.dot(fout_rows[mine, :], hidden, precision=HIGH, preferred_element_type=F32)
        fall = -decay_cols[mine, :]
        for q in range(stretch // RADIX):
            lanes = slice(q * RADIX, (q + 1) * RADIX)
            row = pl.multiple_of((step * (stretch // RADIX) + q) * channels, channels)
            grid32[pl.ds(row, channels), :] = shaped[:, lanes] * jnp.exp(fall * pos[:, lanes])
        return carry

    loads[0].wait()
    project(0)
    pl.semaphore_wait(barrier, 2 * n_seq + 1)
    each_peer(lambda p: project_copy(0, p).start())
    loads[3].wait()
    project(2)
    each_peer(lambda p: project_copy(2, p).start())
    out.start_weights(range(3))
    loads[4].wait()
    project(1)
    each_peer(lambda p: project_copy(1, p).start())
    out.start_weights(range(3, out.n_z))
    out.load_weights()
    for g in range(3):
        own_piece(send4.at[g], pro_recv.at[g])
    for copy in loads[5:]:
        copy.wait()

    lax.fori_loop(0, length // stretch, filter_block, 0)
    forward(grid32, x_all, a_all, rows_all, outer, twist, inner, imp_spec, channels)

    take_projected(0)
    take_projected(2)

    def source_block(row):
        grid32[pl.ds(row, block), :] = mixed(0, row, block) * mixed(2, row, block)

    each_block(source_block)
    forward(grid32, x_all, a_all, rows_all, outer, twist, inner, src_spec, channels)

    for c in range(channels):
        line = slice(c * HALF, (c + 1) * HALF)
        sre, sim = src_spec[line, :RADIX], src_spec[line, RADIX:]
        ire, iim = imp_spec[line, :RADIX], imp_spec[line, RADIX:]
        rows_all[line, :RADIX] = (sre * ire - sim * iim).astype(BF)
        rows_all[line, RADIX:] = (sre * iim + sim * ire).astype(BF)
    src_spec[...] = jnp.dot(rows_all[...], inner_back[...], preferred_element_type=F32)
    co, si = twist[0], twist[1]
    for c in range(channels):
        line = slice(c * HALF, (c + 1) * HALF)
        lanes = slice(c * RADIX, (c + 1) * RADIX)
        re, im = src_spec[line, :RADIX], src_spec[line, RADIX:]
        back = jnp.concatenate([re * co - im * si, im * co + re * si], 0).astype(BF)
        y = jnp.dot(outer_back[...], back, preferred_element_type=F32)
        grid32[pl.ds(c, points, stride=channels), :] = y
    take_projected(1)

    def gate_block(row):
        value = grid32[pl.ds(row, block), :] * mixed(1, row, block)
        gated_send[pl.ds(row // channels, 8)] = value.astype(BF).reshape(8, channels, RADIX)

    each_block(gate_block)

    few = per // 2

    def gated_copy(side, part, peer):
        return pltpu.make_async_remote_copy(
            src_ref=gated_send.at[pl.ds(peer * per + part * few, few)],
            dst_ref=gated.at[side, part * few : (part + 1) * few, mine, :],
            send_sem=gat_ssem.at[side, part, peer],
            recv_sem=gat_rsem.at[side, part, me],
            device_id=(peer, out.across if side else out.c),
            device_id_type=MESH,
        )

    def gated_arrive(side, part, peer):
        piece = gated.at[
            side, part * few : (part + 1) * few, pl.ds(pl.multiple_of(peer * channels, channels), channels), :
        ]
        return pltpu.make_async_remote_copy(
            src_ref=piece, dst_ref=piece, send_sem=gat_ssem.at[side, part, peer], recv_sem=gat_rsem.at[side, part, peer],
            device_id=(peer, out.across if side else out.c), device_id_type=MESH,
        )

    for part in (0, 1):

        def both_sides(p):
            gated_copy(0, part, p).start()
            gated_copy(1, part, p).start()

        each_peer(both_sides)
        gated_copy(1, part, me).start()
    gated[0, :, mine, :] = gated_send[pl.ds(me * per, per)]
    out.pass_weights(range(3))

    def take_gated(part):
        for side in (0, 1):
            each_peer(lambda p: gated_arrive(side, part, p).wait_recv())
            if side:
                gated_arrive(1, part, me).wait_recv()
            for q in range(part * few, (part + 1) * few):
                out.g2[side, q * RADIX : (q + 1) * RADIX, :] = gated[side, q].astype(F32).T.astype(BF)

    out.finish(take_gated)

    for g in range(3):
        each_peer(lambda p: project_copy(g, p).wait_send())
    for part in (0, 1):
        for side in (0, 1):
            each_peer(lambda p: gated_copy(side, part, p).wait_send())
        gated_copy(1, part, me).wait_send()


def operator_rows(
    n_seq, n_ch, tokens, in_weight, short_taps, band_freq, filter_first, filter_bias, filter_out, decay, out_weight
):
    rows, width = tokens.shape
    slab = in_weight.shape[2]
    channels = slab // n_seq
    per = rows // RADIX
    points = per * n_seq
    tables = dft_tables(points)
    anyspec = pl.BlockSpec(memory_space=pl.ANY)
    vspec = pl.BlockSpec(memory_space=pltpu.VMEM)
    dma = pltpu.SemaphoreType.DMA
    scratch = [
        pltpu.VMEM((rows, width), BF),
        pltpu.VMEM((3, width, slab), BF),
        *[pltpu.VMEM(t.shape, t.dtype) for t in tables],
        pltpu.VMEM((3, 3, slab, RADIX), F32),
        pltpu.VMEM((slab, filter_out.shape[0]), F32),
        pltpu.VMEM((slab, RADIX), F32),
        pltpu.VMEM((3, (points + 1) * channels, RADIX), F32),
        pltpu.VMEM((3, per, slab, RADIX), BF),
        pltpu.VMEM((3, points, channels, RADIX), BF),
        pltpu.VMEM((points, channels, RADIX), BF),
        pltpu.VMEM((2, per, slab, RADIX), BF),
        pltpu.VMEM((points * channels, RADIX), F32),
        pltpu.VMEM((points, channels * RADIX), BF),
        pltpu.VMEM((2 * HALF, channels * RADIX), F32),
        pltpu.VMEM((channels * HALF, 2 * RADIX), BF),
        pltpu.VMEM((channels * HALF, 2 * RADIX), F32),
        pltpu.VMEM((channels * HALF, 2 * RADIX), F32),
        dma((10,)), dma((3, n_seq)), dma((3, n_seq)), dma((2, 2, n_seq)), dma((2, 2, n_seq)),
        *spread_scratch(n_ch, rows, slab, out_weight.shape[1] // n_ch),
    ]
    return pl.pallas_call(
        functools.partial(operator_kernel, n_seq, n_ch),
        out_shape=jax.ShapeDtypeStruct((rows, slab), BF),
        in_specs=[anyspec] * 2 + [vspec] * 6 + [anyspec] * 6,
        out_specs=vspec,
        scratch_shapes=scratch,
        compiler_params=pltpu.CompilerParams(collective_id=0, has_side_effects=True, vmem_limit_bytes=56 * 2**20),
        cost_estimate=pl.CostEstimate(flops=2 * rows * width * slab * 3, bytes_accessed=12 * 2**20, transcendentals=0),
    )(
        tokens, jnp.transpose(in_weight, (1, 0, 2)), short_taps, band_freq[None, :], filter_first, filter_bias[None, :],
        filter_out, decay[None, :], *tables, out_weight,
    )


def local(tokens, in_weight, short_taps, band_freq, filter_first, filter_bias, filter_out, decay, out_weight):
    return operator_rows(
        lax.axis_size("seq"), lax.axis_size("ch"), tokens, in_weight, short_taps, band_freq, filter_first, filter_bias,
        filter_out, decay, out_weight,
    )


def solution(mesh):
    in_specs = (
        P("seq", None),
        P(None, None, "ch"),
        P(None, None, "ch"),
        P(),
        P(),
        P(),
        P(None, "ch"),
        P("ch"),
        P("ch", None),
    )
    out_specs = P("seq", "ch")
    return jax.shard_map(local, mesh=mesh, in_specs=in_specs, out_specs=out_specs, check_vma=False)
```

```python
import functools
import math

import jax
import jax.numpy as jnp
import numpy as np
from jax import lax
from jax.experimental import pallas as pl
from jax.experimental.pallas import tpu as pltpu
from jax.sharding import PartitionSpec as P

MESH = pl.DeviceIdType.MESH
BF = jnp.bfloat16
F32 = jnp.float32
HIGH = lax.Precision.HIGHEST
RADIX = 128
HALF = 80


def dft_tables(rows_in):
    full = RADIX * RADIX
    k1 = np.arange(HALF)[:, None]
    used = (k1 <= RADIX // 2).astype(np.float64)
    line = np.arange(RADIX)
    a = 2 * np.pi * k1 * np.arange(rows_in)[None, :] / RADIX
    outer = np.concatenate([np.cos(a) * used, -np.sin(a) * used], 0)
    tw = 2 * np.pi * k1 * line[None, :] / full
    twist = np.stack([np.cos(tw), np.sin(tw)])
    b = 2 * np.pi * np.outer(line, line) / RADIX
    co, si = np.cos(b), np.sin(b)
    inner = np.block([[co, -si], [si, co]])
    inner_back = np.block([[co, si], [-si, co]])
    weight = np.where((k1 == 0) | (k1 == RADIX // 2), 1.0, 2.0) * used / full
    outer_back = np.concatenate([(np.cos(a) * weight).T, (-np.sin(a) * weight).T], 1)
    return (
        jnp.asarray(outer, BF),
        jnp.asarray(twist, F32),
        jnp.asarray(inner, BF),
        jnp.asarray(inner_back, BF),
        jnp.asarray(outer_back, BF),
    )


def sin_turns(turns):
    turns = turns - 0.25
    turns = turns - jnp.round(turns)
    x = (0.25 - jnp.abs(turns)) * (2.0 * math.pi)
    x2 = x * x
    p = jnp.float32(-2.50521083854e-8)
    for c in (2.75573192239858e-6, -1.98412698412698e-4, 8.33333333333333e-3, -1.66666666666667e-1):
        p = p * x2 + jnp.float32(c)
    return x + x * x2 * p


def first_row(v):
    row = lax.broadcasted_iota(jnp.int32, (8, v.shape[1]), 0)
    return jnp.where(row == 0, jnp.broadcast_to(v, (8, v.shape[1])), 0.0)


def contract_rows(a, b):
    return lax.dot_general(a, b, (((0,), (0,)), ((), ())), precision=HIGH, preferred_element_type=F32)


def outer_product(v, w):
    return contract_rows(first_row(v), first_row(w))


def forward(grid32, x_all, a_all, rows_all, outer, twist, inner, spec_ref, channels):
    rows_in = x_all.shape[0]
    for c in range(channels):
        x_all[:, c * RADIX : (c + 1) * RADIX] = grid32[pl.ds(c, rows_in, stride=channels), :].astype(BF)
    a_all[...] = jnp.dot(outer[...], x_all[...], preferred_element_type=F32)
    co, si = twist[0], twist[1]
    for c in range(channels):
        lanes = slice(c * RADIX, (c + 1) * RADIX)
        re, im = a_all[:HALF, lanes], a_all[HALF:, lanes]
        rows = slice(c * HALF, (c + 1) * HALF)
        rows_all[rows, :RADIX] = (re * co + im * si).astype(BF)
        rows_all[rows, RADIX:] = (im * co - re * si).astype(BF)
    spec_ref[...] = jnp.dot(rows_all[...], inner[...], preferred_element_type=F32)


CHUNK = 256


class Spread:
    def __init__(self, n_ch, w_hbm, out_ref, wout, g2, sums, landed, wl_sem, wx_ssem, wx_rsem, wc_ssem, wc_rsem, r_ssem, r_rsem):
        self.__dict__.update(locals())
        del self.__dict__["self"]
        self.n_z = n_ch // 2
        self.c = lax.axis_index("ch")
        self.z = self.c // 2
        self.xl = lax.rem(self.c, 2)
        self.s = lax.axis_index("seq")
        self.core = lax.rem(self.s, 2)
        self.across = self.c + 1 - 2 * self.xl
        far = lax.rem(self.s // 2, 2)
        self.sides = [(self.s, self.across), (self.s + 2 - 4 * far, self.across)]
        self.sibling = {"seq": self.s + 1 - 2 * self.core}
        self.up = {"ch": lax.rem(self.c + 2, n_ch)}
        self.down = {"ch": lax.rem(self.c + n_ch - 2, n_ch)}
        self.depth = w_hbm.shape[0]
        self.cols = w_hbm.shape[1] // n_ch
        self.rows = out_ref.shape[0]
        self.chunks = self.rows // CHUNK
        half = self.n_z // 2
        shifts = [half] + [x for k in range(half - 1, 0, -1) for x in (k, self.n_z - k)] + [0]
        self.need = [lax.rem(self.z + k, self.n_z) for k in shifts]

    def _columns(self, block):
        return pl.ds(pl.multiple_of(block * self.cols, self.cols), self.cols)

    def own_weight(self, j):
        return pltpu.make_async_copy(
            self.w_hbm.at[:, self._columns(2 * j + self.xl)], self.wout.at[0, j], self.wl_sem.at[j]
        )

    def weight_to_side(self, k, side):
        j = self.need[k]
        part = self.depth // 4
        line = pl.ds(pl.multiple_of(self.core * 2 * part + side * part, part), part)
        return pltpu.make_async_remote_copy(
            src_ref=self.w_hbm.at[line, self._columns(2 * j + 1 - self.xl)],
            dst_ref=self.wout.at[1, j, line, :],
            send_sem=self.wx_ssem.at[side, k], recv_sem=self.wx_rsem.at[side, k],
            device_id=self.sides[side], device_id_type=MESH,
        )

    def weight_to_sibling(self, k, core):
        half = self.depth // 2
        piece = self.wout.at[1, self.need[k], pl.ds(pl.multiple_of(core * half, half), half), :]
        return pltpu.make_async_remote_copy(
            src_ref=piece, dst_ref=piece, send_sem=self.wc_ssem.at[k], recv_sem=self.wc_rsem.at[k],
            device_id=self.sibling, device_id_type=MESH,
        )

    def start_weights(self, blocks):
        for k in blocks:
            for side in (0, 1):
                self.weight_to_side(k, side).start()

    def load_weights(self):
        for j in range(self.n_z):
            self.own_weight(j).start()

    def pass_weights(self, blocks):
        for k in blocks:
            for side in (0, 1):
                self.weight_to_side(k, side).wait()
            self.weight_to_sibling(k, self.core).start()

    def take_weights(self, blocks):
        for k in blocks:
            self.weight_to_sibling(k, self.core).wait_send()
            self.weight_to_sibling(k, 1 - self.core).wait_recv()

    def hop(self, way, step, i):
        return pltpu.make_async_remote_copy(
            src_ref=self.sums.at[way, step, i], dst_ref=self.landed.at[way, step, i],
            send_sem=self.r_ssem.at[way, step, i], recv_sem=self.r_rsem.at[way, step, i],
            device_id=(self.up, self.down)[way], device_id_type=MESH,
        )

    def partial_sum(self, block, i):
        line = pl.ds(pl.multiple_of(i * CHUNK, CHUNK), CHUNK)
        return jnp.dot(self.g2[0, line], self.wout[0, block], preferred_element_type=F32) + jnp.dot(
            self.g2[1, line], self.wout[1, block], preferred_element_type=F32
        )

    def block_at(self, way, step):
        n = self.n_z
        if way == 0:
            return lax.rem(self.z + n // 2 - step, n)
        return lax.rem(self.z + n // 2 + step, n)

    def send(self, way, step, i, fresh):
        own = self.partial_sum(self.block_at(way, step), i)
        if not fresh:
            self.hop(way, step - 1, i).wait_recv()
            own = own + self.landed[way, step - 1, i].astype(F32)
        self.sums[way, step, i] = own.astype(BF)
        self.hop(way, step, i).start()

    def finish(self, take_gated):
        for j in range(self.n_z):
            self.own_weight(j).wait()
        half = self.chunks // 2

        def both(steps, firsts, fresh):
            def body(i, carry):
                for way in (0, 1):
                    self.send(way, steps[way], i if firsts[way] else half + i, fresh)
                return carry

            lax.fori_loop(0, half, body, 0)

        self.take_weights([0, 1, 2])
        take_gated(0)
        both((0, 1), (True, True), True)
        take_gated(1)
        both((1, 0), (False, False), True)
        self.pass_weights(range(3, self.n_z))
        both((1, 1), (True, False), False)
        steps = self.n_z // 2
        for step in range(2, steps):
            self.take_weights([2 * step - 1, 2 * step])
            both((step, step), (False, True), False)
            both((step, step), (True, False), False)
        self.take_weights([self.n_z - 1])

        def home(i, carry):
            own = self.partial_sum(self.z, i)
            self.hop(0, steps - 1, i).wait_recv()
            self.hop(1, steps - 1, i).wait_recv()
            own = own + self.landed[0, steps - 1, i].astype(F32) + self.landed[1, steps - 1, i].astype(F32)
            self.out_ref[pl.ds(pl.multiple_of(i * CHUNK, CHUNK), CHUNK), :] = own.astype(BF)
            return carry

        lax.fori_loop(0, self.chunks, home, 0)

        def drain(i, carry):
            for step in range(1, steps):
                self.hop(0, step, i).wait_send()
                self.hop(1, step, i).wait_send()
            return carry

        lax.fori_loop(0, self.chunks, drain, 0)

        def drain_first(i, carry):
            self.hop(0, 0, i).wait_send()
            self.hop(1, 0, half + i).wait_send()
            return carry

        lax.fori_loop(0, half, drain_first, 0)


def spread_scratch(n_ch, rows, depth, cols):
    n_z = n_ch // 2
    dma = pltpu.SemaphoreType.DMA
    return [
        pltpu.VMEM((2, n_z, depth, cols), BF),
        pltpu.VMEM((2, rows, depth), BF),
        pltpu.VMEM((2, n_z // 2, rows // CHUNK, CHUNK, cols), BF),
        pltpu.VMEM((2, n_z // 2, rows // CHUNK, CHUNK, cols), BF),
        dma((n_z,)), dma((2, n_z)), dma((2, n_z)), dma((n_z,)), dma((n_z,)),
        dma((2, n_z // 2, rows // CHUNK)), dma((2, n_z // 2, rows // CHUNK)),
    ]


def operator_kernel(
    n_seq, n_ch,
    tok_hbm, w_hbm, taps, band, first, bias, fout, decay, outer_hbm, twist_hbm, inner_hbm, inner_back_hbm, outer_back_hbm, wout_hbm,
    out_ref,
    tok, w, outer, twist, inner, inner_back, outer_back,
    tap_cols, fout_rows, decay_cols, padded, send4, pro_recv, gated_send, gated,
    grid32, x_all, a_all, rows_all, imp_spec, src_spec,
    load_sem, pro_ssem, pro_rsem, gat_ssem, gat_rsem, *out_scratch,
):
    me = lax.axis_index("seq")
    out = Spread(n_ch, wout_hbm, out_ref, *out_scratch)
    rows, width = tok_hbm.shape
    slab = w_hbm.shape[2]
    channels = slab // n_seq
    per = rows // RADIX
    points = per * n_seq
    half = rows // 2
    length = rows * n_seq

    loads = [
        pltpu.make_async_copy(w_hbm.at[0], w.at[0], load_sem.at[0]),
        pltpu.make_async_copy(tok_hbm.at[:half], tok.at[:half], load_sem.at[1]),
        pltpu.make_async_copy(tok_hbm.at[half:], tok.at[half:], load_sem.at[2]),
        pltpu.make_async_copy(w_hbm.at[2], w.at[2], load_sem.at[3]),
        pltpu.make_async_copy(w_hbm.at[1], w.at[1], load_sem.at[4]),
        pltpu.make_async_copy(outer_hbm, outer, load_sem.at[5]),
        pltpu.make_async_copy(twist_hbm, twist, load_sem.at[6]),
        pltpu.make_async_copy(inner_hbm, inner, load_sem.at[7]),
        pltpu.make_async_copy(inner_back_hbm, inner_back, load_sem.at[8]),
        pltpu.make_async_copy(outer_back_hbm, outer_back, load_sem.at[9]),
    ]
    for copy in loads:
        copy.start()

    barrier = pltpu.get_barrier_semaphore()

    def greet(d, carry):
        pl.semaphore_signal(barrier, inc=1, device_id={"seq": lax.rem(me + d, n_seq)}, device_id_type=MESH)
        return carry

    lax.fori_loop(1, n_seq, greet, 0)

    def greet_across(p, carry):
        pl.semaphore_signal(barrier, inc=1, device_id=(p, out.across), device_id_type=MESH)
        return carry

    lax.fori_loop(0, n_seq, greet_across, 0)
    for peer in (out.up, out.down):
        pl.semaphore_signal(barrier, inc=1, device_id=peer, device_id_type=MESH)

    for g in range(3):
        for i in range(3):
            tap_cols[g, i] = jnp.broadcast_to(taps[i, g : g + 1, :], (RADIX, slab)).T
        padded[g, 0:channels, :] = jnp.zeros((channels, RADIX), F32)
    fout_rows[...] = fout[...].T
    decay_cols[...] = jnp.broadcast_to(decay[...], (RADIX, slab)).T

    mine = pl.ds(pl.multiple_of(me * channels, channels), channels)

    def spread_copy(src, dst, ssem, rsem, peer):
        return pltpu.make_async_remote_copy(
            src_ref=src.at[peer],
            dst_ref=dst.at[pl.ds(me * per, per)],
            send_sem=ssem.at[peer],
            recv_sem=rsem.at[me],
            device_id={"seq": peer},
            device_id_type=MESH,
        )

    def arrive(dst, ssem, rsem, peer):
        piece = dst.at[pl.ds(peer * per, per)]
        return pltpu.make_async_remote_copy(
            src_ref=piece, dst_ref=piece, send_sem=ssem.at[peer], recv_sem=rsem.at[peer],
            device_id={"seq": peer}, device_id_type=MESH,
        )

    def own_piece(src, dst):
        dst[pl.ds(me * per, per)] = src[me]

    def each_peer(step):
        def body(d, carry):
            step(lax.rem(me + d, n_seq))
            return carry

        lax.fori_loop(1, n_seq, body, 0)

    def project(g):
        for part in (0, 1):
            if g == 0:
                loads[1 + part].wait()
            y = jnp.dot(tok[part * half : (part + 1) * half, :], w[g], preferred_element_type=F32)
            for q in range(per // 2):
                piece = y[q * RADIX : (q + 1) * RADIX, :].T.astype(BF)
                send4[g, :, part * (per // 2) + q] = piece.reshape(n_seq, channels, RADIX)

    def project_copy(g, p):
        return spread_copy(send4.at[g], pro_recv.at[g], pro_ssem.at[g], pro_rsem.at[g], p)

    def mixed(g, row, count):
        lane = lax.broadcasted_iota(jnp.int32, (count, RADIX), 1)
        now = padded[g, pl.ds(channels + row, count), :]
        before = padded[g, pl.ds(row, count), :]
        total = jnp.zeros((count // channels, channels, RADIX), F32)
        for i in range(3):
            moved = now if i == 0 else pltpu.roll(jnp.where(lane >= RADIX - i, before, now), i, 1)
            total = total + tap_cols[g, i, mine, :][None] * moved.reshape(count // channels, channels, RADIX)
        return total.reshape(count, RADIX)

    def take_projected(g):
        each_peer(lambda p: arrive(pro_recv.at[g], pro_ssem.at[g], pro_rsem.at[g], p).wait_recv())
        padded[g, channels:, :] = pro_recv[g].astype(F32).reshape(points * channels, RADIX)

    block = 8 * channels

    def each_block(step):
        def body(i, carry):
            step(pl.multiple_of(i * block, block))
            return carry

        lax.fori_loop(0, points * channels // block, body, 0)

    n_band = band.shape[1]
    stretch = 2 * rows

    def filter_block(step, carry):
        pos = (step * stretch + lax.broadcasted_iota(jnp.int32, (1, stretch), 1)).astype(F32)
        scaled = pos * (1.0 / length)
        turns = outer_product(band[...], scaled)
        turns = turns - jnp.round(turns)
        head = lax.broadcasted_iota(jnp.int32, (8, stretch), 0)
        features = jnp.concatenate(
            [sin_turns(turns + 0.25), sin_turns(turns), jnp.where(head == 0, scaled, jnp.where(head == 1, 1.0, 0.0))], 0
        )
        head = lax.broadcasted_iota(jnp.int32, (8, first.shape[1]), 0)
        layer = jnp.concatenate(
            [
                first[1 : 1 + n_band, :],
                first[1 + n_band :, :],
                jnp.where(head == 0, first[0:1, :], jnp.where(head == 1, bias[...], 0.0)),
            ],
            0,
        )
        hidden = sin_turns(contract_rows(layer, features) * (1.0 / (2.0 * math.pi)))
        shaped = jnp.dot(fout_rows[mine, :], hidden, precision=HIGH, preferred_element_type=F32)
        fall = -decay_cols[mine, :]
        for q in range(stretch // RADIX):
            lanes = slice(q * RADIX, (q + 1) * RADIX)
            row = pl.multiple_of((step * (stretch // RADIX) + q) * channels, channels)
            grid32[pl.ds(row, channels), :] = shaped[:, lanes] * jnp.exp(fall * pos[:, lanes])
        return carry

    loads[0].wait()
    project(0)
    pl.semaphore_wait(barrier, 2 * n_seq + 1)
    each_peer(lambda p: project_copy(0, p).start())
    loads[3].wait()
    project(2)
    each_peer(lambda p: project_copy(2, p).start())
    out.start_weights(range(3))
    loads[4].wait()
    project(1)
    each_peer(lambda p: project_copy(1, p).start())
    out.start_weights(range(3, out.n_z))
    out.load_weights()
    for g in range(3):
        own_piece(send4.at[g], pro_recv.at[g])
    for copy in loads[5:]:
        copy.wait()

    lax.fori_loop(0, length // stretch, filter_block, 0)
    forward(grid32, x_all, a_all, rows_all, outer, twist, inner, imp_spec, channels)

    take_projected(0)
    take_projected(2)

    def source_block(row):
        grid32[pl.ds(row, block), :] = mixed(0, row, block) * mixed(2, row, block)

    each_block(source_block)
    forward(grid32, x_all, a_all, rows_all, outer, twist, inner, src_spec, channels)

    for c in range(channels):
        line = slice(c * HALF, (c + 1) * HALF)
        sre, sim = src_spec[line, :RADIX], src_spec[line, RADIX:]
        ire, iim = imp_spec[line, :RADIX], imp_spec[line, RADIX:]
        rows_all[line, :RADIX] = (sre * ire - sim * iim).astype(BF)
        rows_all[line, RADIX:] = (sre * iim + sim * ire).astype(BF)
    src_spec[...] = jnp.dot(rows_all[...], inner_back[...], preferred_element_type=F32)
    co, si = twist[0], twist[1]
    for c in range(channels):
        line = slice(c * HALF, (c + 1) * HALF)
        lanes = slice(c * RADIX, (c + 1) * RADIX)
        re, im = src_spec[line, :RADIX], src_spec[line, RADIX:]
        back = jnp.concatenate([re * co - im * si, im * co + re * si], 0).astype(BF)
        y = jnp.dot(outer_back[...], back, preferred_element_type=F32)
        grid32[pl.ds(c, points, stride=channels), :] = y
    take_projected(1)

    def gate_block(row):
        value = grid32[pl.ds(row, block), :] * mixed(1, row, block)
        gated_send[pl.ds(row // channels, 8)] = value.astype(BF).reshape(8, channels, RADIX)

    each_block(gate_block)

    few = per // 2

    def gated_copy(side, part, peer):
        return pltpu.make_async_remote_copy(
            src_ref=gated_send.at[pl.ds(peer * per + part * few, few)],
            dst_ref=gated.at[side, me, part * few : (part + 1) * few],
            send_sem=gat_ssem.at[side, part, peer],
            recv_sem=gat_rsem.at[side, part, me],
            device_id=(peer, out.across if side else out.c),
            device_id_type=MESH,
        )

    def gated_arrive(side, part, peer):
        piece = gated.at[side, peer, part * few : (part + 1) * few]
        return pltpu.make_async_remote_copy(
            src_ref=piece, dst_ref=piece, send_sem=gat_ssem.at[side, part, peer], recv_sem=gat_rsem.at[side, part, peer],
            device_id=(peer, out.across if side else out.c), device_id_type=MESH,
        )

    for part in (0, 1):

        def both_sides(p):
            gated_copy(0, part, p).start()
            gated_copy(1, part, p).start()

        each_peer(both_sides)
        gated_copy(1, part, me).start()
    gated[0, me] = gated_send[pl.ds(me * per, per)]
    out.pass_weights(range(3))

    def take_gated(part):
        for side in (0, 1):
            each_peer(lambda p: gated_arrive(side, part, p).wait_recv())
            if side:
                gated_arrive(1, part, me).wait_recv()
            for q in range(part * few, (part + 1) * few):
                rows_first = gated[side, :, q].reshape(slab, RADIX).astype(F32)
                out.g2[side, q * RADIX : (q + 1) * RADIX, :] = rows_first.T.astype(BF)

    out.finish(take_gated)

    for g in range(3):
        each_peer(lambda p: project_copy(g, p).wait_send())
    for part in (0, 1):
        for side in (0, 1):
            each_peer(lambda p: gated_copy(side, part, p).wait_send())
        gated_copy(1, part, me).wait_send()


def operator_rows(
    n_seq, n_ch, tokens, in_weight, short_taps, band_freq, filter_first, filter_bias, filter_out, decay, out_weight
):
    rows, width = tokens.shape
    slab = in_weight.shape[2]
    channels = slab // n_seq
    per = rows // RADIX
    points = per * n_seq
    tables = dft_tables(points)
    anyspec = pl.BlockSpec(memory_space=pl.ANY)
    vspec = pl.BlockSpec(memory_space=pltpu.VMEM)
    dma = pltpu.SemaphoreType.DMA
    scratch = [
        pltpu.VMEM((rows, width), BF),
        pltpu.VMEM((3, width, slab), BF),
        *[pltpu.VMEM(t.shape, t.dtype) for t in tables],
        pltpu.VMEM((3, 3, slab, RADIX), F32),
        pltpu.VMEM((slab, filter_out.shape[0]), F32),
        pltpu.VMEM((slab, RADIX), F32),
        pltpu.VMEM((3, (points + 1) * channels, RADIX), F32),
        pltpu.VMEM((3, n_seq, per, channels, RADIX), BF),
        pltpu.VMEM((3, points, channels, RADIX), BF),
        pltpu.VMEM((points, channels, RADIX), BF),
        pltpu.VMEM((2, n_seq, per, channels, RADIX), BF),
        pltpu.VMEM((points * channels, RADIX), F32),
        pltpu.VMEM((points, channels * RADIX), BF),
        pltpu.VMEM((2 * HALF, channels * RADIX), F32),
        pltpu.VMEM((channels * HALF, 2 * RADIX), BF),
        pltpu.VMEM((channels * HALF, 2 * RADIX), F32),
        pltpu.VMEM((channels * HALF, 2 * RADIX), F32),
        dma((10,)), dma((3, n_seq)), dma((3, n_seq)), dma((2, 2, n_seq)), dma((2, 2, n_seq)),
        *spread_scratch(n_ch, rows, slab, out_weight.shape[1] // n_ch),
    ]
    return pl.pallas_call(
        functools.partial(operator_kernel, n_seq, n_ch),
        out_shape=jax.ShapeDtypeStruct((rows, slab), BF),
        in_specs=[anyspec] * 2 + [vspec] * 6 + [anyspec] * 6,
        out_specs=vspec,
        scratch_shapes=scratch,
        compiler_params=pltpu.CompilerParams(collective_id=0, has_side_effects=True, vmem_limit_bytes=56 * 2**20),
        cost_estimate=pl.CostEstimate(flops=2 * rows * width * slab * 3, bytes_accessed=12 * 2**20, transcendentals=0),
    )(
        tokens, jnp.transpose(in_weight, (1, 0, 2)), short_taps, band_freq[None, :], filter_first, filter_bias[None, :],
        filter_out, decay[None, :], *tables, out_weight,
    )


def local(tokens, in_weight, short_taps, band_freq, filter_first, filter_bias, filter_out, decay, out_weight):
    return operator_rows(
        lax.axis_size("seq"), lax.axis_size("ch"), tokens, in_weight, short_taps, band_freq, filter_first, filter_bias,
        filter_out, decay, out_weight,
    )


def solution(mesh):
    in_specs = (
        P("seq", None),
        P(None, None, "ch"),
        P(None, None, "ch"),
        P(),
        P(),
        P(),
        P(None, "ch"),
        P("ch"),
        P("ch", None),
    )
    out_specs = P("seq", "ch")
    return jax.shard_map(local, mesh=mesh, in_specs=in_specs, out_specs=out_specs, check_vma=False)
```

```python
import functools
import math

import jax
import jax.numpy as jnp
import numpy as np
from jax import lax
from jax.experimental import pallas as pl
from jax.experimental.pallas import tpu as pltpu
from jax.sharding import PartitionSpec as P

MESH = pl.DeviceIdType.MESH
BF = jnp.bfloat16
F32 = jnp.float32
HIGH = lax.Precision.HIGHEST
RADIX = 128
HALF = 80


def dft_tables(rows_in):
    full = RADIX * RADIX
    k1 = np.arange(HALF)[:, None]
    used = (k1 <= RADIX // 2).astype(np.float64)
    line = np.arange(RADIX)
    a = 2 * np.pi * k1 * np.arange(rows_in)[None, :] / RADIX
    outer = np.concatenate([np.cos(a) * used, -np.sin(a) * used], 0)
    tw = 2 * np.pi * k1 * line[None, :] / full
    twist = np.stack([np.cos(tw), np.sin(tw)])
    b = 2 * np.pi * np.outer(line, line) / RADIX
    co, si = np.cos(b), np.sin(b)
    inner = np.block([[co, -si], [si, co]])
    inner_back = np.block([[co, si], [-si, co]])
    weight = np.where((k1 == 0) | (k1 == RADIX // 2), 1.0, 2.0) * used / full
    outer_back = np.concatenate([(np.cos(a) * weight).T, (-np.sin(a) * weight).T], 1)
    return (
        jnp.asarray(outer, BF),
        jnp.asarray(twist, F32),
        jnp.asarray(inner, BF),
        jnp.asarray(inner_back, BF),
        jnp.asarray(outer_back, BF),
    )


def sin_turns(turns):
    turns = turns - 0.25
    turns = turns - jnp.round(turns)
    x = (0.25 - jnp.abs(turns)) * (2.0 * math.pi)
    x2 = x * x
    p = jnp.float32(-2.50521083854e-8)
    for c in (2.75573192239858e-6, -1.98412698412698e-4, 8.33333333333333e-3, -1.66666666666667e-1):
        p = p * x2 + jnp.float32(c)
    return x + x * x2 * p


def first_row(v):
    row = lax.broadcasted_iota(jnp.int32, (8, v.shape[1]), 0)
    return jnp.where(row == 0, jnp.broadcast_to(v, (8, v.shape[1])), 0.0)


def contract_rows(a, b):
    return lax.dot_general(a, b, (((0,), (0,)), ((), ())), precision=HIGH, preferred_element_type=F32)


def outer_product(v, w):
    return contract_rows(first_row(v), first_row(w))


def forward(grid32, x_all, a_all, rows_all, outer, twist, inner, spec_ref, channels):
    rows_in = x_all.shape[0]
    for c in range(channels):
        x_all[:, c * RADIX : (c + 1) * RADIX] = grid32[pl.ds(c, rows_in, stride=channels), :].astype(BF)
    a_all[...] = jnp.dot(outer[...], x_all[...], preferred_element_type=F32)
    co, si = twist[0], twist[1]
    for c in range(channels):
        lanes = slice(c * RADIX, (c + 1) * RADIX)
        re, im = a_all[:HALF, lanes], a_all[HALF:, lanes]
        rows = slice(c * HALF, (c + 1) * HALF)
        rows_all[rows, :RADIX] = (re * co + im * si).astype(BF)
        rows_all[rows, RADIX:] = (im * co - re * si).astype(BF)
    spec_ref[...] = jnp.dot(rows_all[...], inner[...], preferred_element_type=F32)


CHUNK = 256


class Spread:
    def __init__(self, n_ch, w_hbm, out_ref, wout, g2, sums, landed, wl_sem, wx_ssem, wx_rsem, wc_ssem, wc_rsem, r_ssem, r_rsem):
        self.__dict__.update(locals())
        del self.__dict__["self"]
        self.n_z = n_ch // 2
        self.c = lax.axis_index("ch")
        self.z = self.c // 2
        self.xl = lax.rem(self.c, 2)
        self.s = lax.axis_index("seq")
        self.core = lax.rem(self.s, 2)
        self.across = self.c + 1 - 2 * self.xl
        far = lax.rem(self.s // 2, 2)
        self.sides = [(self.s, self.across), (self.s + 2 - 4 * far, self.across)]
        self.sibling = {"seq": self.s + 1 - 2 * self.core}
        self.up = {"ch": lax.rem(self.c + 2, n_ch)}
        self.down = {"ch": lax.rem(self.c + n_ch - 2, n_ch)}
        self.depth = w_hbm.shape[0]
        self.cols = w_hbm.shape[1] // n_ch
        self.rows = out_ref.shape[0]
        self.chunks = self.rows // CHUNK
        half = self.n_z // 2
        shifts = [half] + [x for k in range(half - 1, 0, -1) for x in (k, self.n_z - k)] + [0]
        self.need = [lax.rem(self.z + k, self.n_z) for k in shifts]

    def _columns(self, block):
        return pl.ds(pl.multiple_of(block * self.cols, self.cols), self.cols)

    def own_weight(self, j):
        return pltpu.make_async_copy(
            self.w_hbm.at[:, self._columns(2 * j + self.xl)], self.wout.at[0, j], self.wl_sem.at[j]
        )

    def weight_to_side(self, k, side):
        j = self.need[k]
        part = self.depth // 4
        line = pl.ds(pl.multiple_of(self.core * 2 * part + side * part, part), part)
        return pltpu.make_async_remote_copy(
            src_ref=self.w_hbm.at[line, self._columns(2 * j + 1 - self.xl)],
            dst_ref=self.wout.at[1, j, line, :],
            send_sem=self.wx_ssem.at[side, k], recv_sem=self.wx_rsem.at[side, k],
            device_id=self.sides[side], device_id_type=MESH,
        )

    def weight_to_sibling(self, k, core):
        half = self.depth // 2
        piece = self.wout.at[1, self.need[k], pl.ds(pl.multiple_of(core * half, half), half), :]
        return pltpu.make_async_remote_copy(
            src_ref=piece, dst_ref=piece, send_sem=self.wc_ssem.at[k], recv_sem=self.wc_rsem.at[k],
            device_id=self.sibling, device_id_type=MESH,
        )

    def start_weights(self, blocks):
        for k in blocks:
            for side in (0, 1):
                self.weight_to_side(k, side).start()

    def load_weights(self):
        for j in range(self.n_z):
            self.own_weight(j).start()

    def pass_weights(self, blocks):
        for k in blocks:
            for side in (0, 1):
                self.weight_to_side(k, side).wait()
            self.weight_to_sibling(k, self.core).start()

    def take_weights(self, blocks):
        for k in blocks:
            self.weight_to_sibling(k, self.core).wait_send()
            self.weight_to_sibling(k, 1 - self.core).wait_recv()

    def hop(self, way, step, i):
        return pltpu.make_async_remote_copy(
            src_ref=self.sums.at[way, step, i], dst_ref=self.landed.at[way, step, i],
            send_sem=self.r_ssem.at[way, step, i], recv_sem=self.r_rsem.at[way, step, i],
            device_id=(self.up, self.down)[way], device_id_type=MESH,
        )

    def partial_sum(self, block, i):
        line = pl.ds(pl.multiple_of(i * CHUNK, CHUNK), CHUNK)
        return jnp.dot(self.g2[0, line], self.wout[0, block], preferred_element_type=F32) + jnp.dot(
            self.g2[1, line], self.wout[1, block], preferred_element_type=F32
        )

    def block_at(self, way, step):
        n = self.n_z
        if way == 0:
            return lax.rem(self.z + n // 2 - step, n)
        return lax.rem(self.z + n // 2 + step, n)

    def send(self, way, step, i, fresh):
        own = self.partial_sum(self.block_at(way, step), i)
        if not fresh:
            self.hop(way, step - 1, i).wait_recv()
            own = own + self.landed[way, step - 1, i].astype(F32)
        self.sums[way, step, i] = own.astype(BF)
        self.hop(way, step, i).start()

    def finish(self, take_gated):
        for j in range(self.n_z):
            self.own_weight(j).wait()
        half = self.chunks // 2

        def both(steps, firsts, fresh):
            def body(i, carry):
                for way in (0, 1):
                    self.send(way, steps[way], i if firsts[way] else half + i, fresh)
                return carry

            lax.fori_loop(0, half, body, 0)

        self.take_weights([0, 1, 2])
        take_gated(0)
        both((0, 1), (True, True), True)
        take_gated(1)
        both((1, 0), (False, False), True)
        self.pass_weights(range(3, self.n_z))
        both((1, 1), (True, False), False)
        steps = self.n_z // 2
        for step in range(2, steps):
            self.take_weights([2 * step - 1, 2 * step])
            both((step, step), (False, True), False)
            both((step, step), (True, False), False)
        self.take_weights([self.n_z - 1])

        def home(i, carry):
            own = self.partial_sum(self.z, i)
            self.hop(0, steps - 1, i).wait_recv()
            self.hop(1, steps - 1, i).wait_recv()
            own = own + self.landed[0, steps - 1, i].astype(F32) + self.landed[1, steps - 1, i].astype(F32)
            self.out_ref[pl.ds(pl.multiple_of(i * CHUNK, CHUNK), CHUNK), :] = own.astype(BF)
            return carry

        lax.fori_loop(0, self.chunks, home, 0)

        def drain(i, carry):
            for step in range(1, steps):
                self.hop(0, step, i).wait_send()
                self.hop(1, step, i).wait_send()
            return carry

        lax.fori_loop(0, self.chunks, drain, 0)

        def drain_first(i, carry):
            self.hop(0, 0, i).wait_send()
            self.hop(1, 0, half + i).wait_send()
            return carry

        lax.fori_loop(0, half, drain_first, 0)


def spread_scratch(n_ch, rows, depth, cols):
    n_z = n_ch // 2
    dma = pltpu.SemaphoreType.DMA
    return [
        pltpu.VMEM((2, n_z, depth, cols), BF),
        pltpu.VMEM((2, rows, depth), BF),
        pltpu.VMEM((2, n_z // 2, rows // CHUNK, CHUNK, cols), BF),
        pltpu.VMEM((2, n_z // 2, rows // CHUNK, CHUNK, cols), BF),
        dma((n_z,)), dma((2, n_z)), dma((2, n_z)), dma((n_z,)), dma((n_z,)),
        dma((2, n_z // 2, rows // CHUNK)), dma((2, n_z // 2, rows // CHUNK)),
    ]


def operator_kernel(
    n_seq, n_ch,
    tok_hbm, w_hbm, taps_hbm, band_hbm, first_hbm, bias_hbm, fout_hbm, decay_hbm, outer_hbm, twist_hbm, inner_hbm, inner_back_hbm, outer_back_hbm, wout_hbm,
    out_ref,
    tok, w, taps, band, first, bias, fout, decay, outer, twist, inner, inner_back, outer_back,
    tap_cols, fout_rows, decay_cols, padded, send4, pro_recv, gated_send, gated,
    grid32, x_all, a_all, rows_all, imp_spec, src_spec,
    load_sem, pro_ssem, pro_rsem, gat_ssem, gat_rsem, *out_scratch,
):
    me = lax.axis_index("seq")
    out = Spread(n_ch, wout_hbm, out_ref, *out_scratch)
    rows, width = tok_hbm.shape
    slab = w_hbm.shape[2]
    channels = slab // n_seq
    per = rows // RADIX
    points = per * n_seq
    half = rows // 2
    length = rows * n_seq

    loads = [
        pltpu.make_async_copy(w_hbm.at[0], w.at[0], load_sem.at[0]),
        pltpu.make_async_copy(tok_hbm.at[:half], tok.at[:half], load_sem.at[1]),
        pltpu.make_async_copy(tok_hbm.at[half:], tok.at[half:], load_sem.at[2]),
        pltpu.make_async_copy(w_hbm.at[2], w.at[2], load_sem.at[3]),
        pltpu.make_async_copy(w_hbm.at[1], w.at[1], load_sem.at[4]),
        pltpu.make_async_copy(outer_hbm, outer, load_sem.at[5]),
        pltpu.make_async_copy(twist_hbm, twist, load_sem.at[6]),
        pltpu.make_async_copy(inner_hbm, inner, load_sem.at[7]),
        pltpu.make_async_copy(inner_back_hbm, inner_back, load_sem.at[8]),
        pltpu.make_async_copy(outer_back_hbm, outer_back, load_sem.at[9]),
    ]
    small = [
        pltpu.make_async_copy(a, b, load_sem.at[10 + i])
        for i, (a, b) in enumerate(
            [(taps_hbm, taps), (fout_hbm, fout), (decay_hbm, decay), (band_hbm, band), (first_hbm, first), (bias_hbm, bias)]
        )
    ]
    for copy in loads[:2] + small + loads[2:]:
        copy.start()

    barrier = pltpu.get_barrier_semaphore()

    def greet(d, carry):
        pl.semaphore_signal(barrier, inc=1, device_id={"seq": lax.rem(me + d, n_seq)}, device_id_type=MESH)
        return carry

    lax.fori_loop(1, n_seq, greet, 0)

    def greet_across(p, carry):
        pl.semaphore_signal(barrier, inc=1, device_id=(p, out.across), device_id_type=MESH)
        return carry

    lax.fori_loop(0, n_seq, greet_across, 0)
    for peer in (out.up, out.down):
        pl.semaphore_signal(barrier, inc=1, device_id=peer, device_id_type=MESH)

    for copy in small:
        copy.wait()
    for g in range(3):
        for i in range(3):
            tap_cols[g, i] = jnp.broadcast_to(taps[i, g : g + 1, :], (RADIX, slab)).T
        padded[g, 0:channels, :] = jnp.zeros((channels, RADIX), F32)
    fout_rows[...] = fout[...].T
    decay_cols[...] = jnp.broadcast_to(decay[...], (RADIX, slab)).T

    mine = pl.ds(pl.multiple_of(me * channels, channels), channels)

    def spread_copy(src, dst, ssem, rsem, peer):
        return pltpu.make_async_remote_copy(
            src_ref=src.at[peer],
            dst_ref=dst.at[pl.ds(me * per, per)],
            send_sem=ssem.at[peer],
            recv_sem=rsem.at[me],
            device_id={"seq": peer},
            device_id_type=MESH,
        )

    def arrive(dst, ssem, rsem, peer):
        piece = dst.at[pl.ds(peer * per, per)]
        return pltpu.make_async_remote_copy(
            src_ref=piece, dst_ref=piece, send_sem=ssem.at[peer], recv_sem=rsem.at[peer],
            device_id={"seq": peer}, device_id_type=MESH,
        )

    def own_piece(src, dst):
        dst[pl.ds(me * per, per)] = src[me]

    def each_peer(step):
        def body(d, carry):
            step(lax.rem(me + d, n_seq))
            return carry

        lax.fori_loop(1, n_seq, body, 0)

    def project(g):
        for part in (0, 1):
            if g == 0:
                loads[1 + part].wait()
            y = jnp.dot(tok[part * half : (part + 1) * half, :], w[g], preferred_element_type=F32)
            for q in range(per // 2):
                piece = y[q * RADIX : (q + 1) * RADIX, :].T.astype(BF)
                send4[g, :, part * (per // 2) + q] = piece.reshape(n_seq, channels, RADIX)

    def project_copy(g, p):
        return spread_copy(send4.at[g], pro_recv.at[g], pro_ssem.at[g], pro_rsem.at[g], p)

    def mixed(g, row, count):
        lane = lax.broadcasted_iota(jnp.int32, (count, RADIX), 1)
        now = padded[g, pl.ds(channels + row, count), :]
        before = padded[g, pl.ds(row, count), :]
        total = jnp.zeros((count // channels, channels, RADIX), F32)
        for i in range(3):
            moved = now if i == 0 else pltpu.roll(jnp.where(lane >= RADIX - i, before, now), i, 1)
            total = total + tap_cols[g, i, mine, :][None] * moved.reshape(count // channels, channels, RADIX)
        return total.reshape(count, RADIX)

    def take_projected(g):
        each_peer(lambda p: arrive(pro_recv.at[g], pro_ssem.at[g], pro_rsem.at[g], p).wait_recv())
        padded[g, channels:, :] = pro_recv[g].astype(F32).reshape(points * channels, RADIX)

    block = 8 * channels

    def each_block(step):
        def body(i, carry):
            step(pl.multiple_of(i * block, block))
            return carry

        lax.fori_loop(0, points * channels // block, body, 0)

    n_band = band.shape[1]
    stretch = 2 * rows

    def filter_block(step, carry):
        pos = (step * stretch + lax.broadcasted_iota(jnp.int32, (1, stretch), 1)).astype(F32)
        scaled = pos * (1.0 / length)
        turns = outer_product(band[...], scaled)
        turns = turns - jnp.round(turns)
        head = lax.broadcasted_iota(jnp.int32, (8, stretch), 0)
        features = jnp.concatenate(
            [sin_turns(turns + 0.25), sin_turns(turns), jnp.where(head == 0, scaled, jnp.where(head == 1, 1.0, 0.0))], 0
        )
        head = lax.broadcasted_iota(jnp.int32, (8, first.shape[1]), 0)
        layer = jnp.concatenate(
            [
                first[1 : 1 + n_band, :],
                first[1 + n_band :, :],
                jnp.where(head == 0, first[0:1, :], jnp.where(head == 1, bias[...], 0.0)),
            ],
            0,
        )
        hidden = sin_turns(contract_rows(layer, features) * (1.0 / (2.0 * math.pi)))
        shaped = jnp.dot(fout_rows[mine, :], hidden, precision=HIGH, preferred_element_type=F32)
        fall = -decay_cols[mine, :]
        for q in range(stretch // RADIX):
            lanes = slice(q * RADIX, (q + 1) * RADIX)
            row = pl.multiple_of((step * (stretch // RADIX) + q) * channels, channels)
            grid32[pl.ds(row, channels), :] = shaped[:, lanes] * jnp.exp(fall * pos[:, lanes])
        return carry

    loads[0].wait()
    project(0)
    pl.semaphore_wait(barrier, 2 * n_seq + 1)
    each_peer(lambda p: project_copy(0, p).start())
    loads[3].wait()
    project(2)
    each_peer(lambda p: project_copy(2, p).start())
    out.start_weights(range(3))
    loads[4].wait()
    project(1)
    each_peer(lambda p: project_copy(1, p).start())
    out.start_weights(range(3, out.n_z))
    out.load_weights()
    for g in range(3):
        own_piece(send4.at[g], pro_recv.at[g])
    for copy in loads[5:]:
        copy.wait()

    lax.fori_loop(0, length // stretch, filter_block, 0)
    forward(grid32, x_all, a_all, rows_all, outer, twist, inner, imp_spec, channels)

    take_projected(0)
    take_projected(2)

    def source_block(row):
        grid32[pl.ds(row, block), :] = mixed(0, row, block) * mixed(2, row, block)

    each_block(source_block)
    forward(grid32, x_all, a_all, rows_all, outer, twist, inner, src_spec, channels)

    for c in range(channels):
        line = slice(c * HALF, (c + 1) * HALF)
        sre, sim = src_spec[line, :RADIX], src_spec[line, RADIX:]
        ire, iim = imp_spec[line, :RADIX], imp_spec[line, RADIX:]
        rows_all[line, :RADIX] = (sre * ire - sim * iim).astype(BF)
        rows_all[line, RADIX:] = (sre * iim + sim * ire).astype(BF)
    src_spec[...] = jnp.dot(rows_all[...], inner_back[...], preferred_element_type=F32)
    co, si = twist[0], twist[1]
    for c in range(channels):
        line = slice(c * HALF, (c + 1) * HALF)
        lanes = slice(c * RADIX, (c + 1) * RADIX)
        re, im = src_spec[line, :RADIX], src_spec[line, RADIX:]
        back = jnp.concatenate([re * co - im * si, im * co + re * si], 0).astype(BF)
        y = jnp.dot(outer_back[...], back, preferred_element_type=F32)
        grid32[pl.ds(c, points, stride=channels), :] = y
    take_projected(1)

    def gate_block(row):
        value = grid32[pl.ds(row, block), :] * mixed(1, row, block)
        gated_send[pl.ds(row // channels, 8)] = value.astype(BF).reshape(8, channels, RADIX)

    each_block(gate_block)

    few = per // 2

    def gated_copy(side, part, peer):
        return pltpu.make_async_remote_copy(
            src_ref=gated_send.at[pl.ds(peer * per + part * few, few)],
            dst_ref=gated.at[side, me, part * few : (part + 1) * few],
            send_sem=gat_ssem.at[side, part, peer],
            recv_sem=gat_rsem.at[side, part, me],
            device_id=(peer, out.across if side else out.c),
            device_id_type=MESH,
        )

    def gated_arrive(side, part, peer):
        piece = gated.at[side, peer, part * few : (part + 1) * few]
        return pltpu.make_async_remote_copy(
            src_ref=piece, dst_ref=piece, send_sem=gat_ssem.at[side, part, peer], recv_sem=gat_rsem.at[side, part, peer],
            device_id=(peer, out.across if side else out.c), device_id_type=MESH,
        )

    for part in (0, 1):

        def both_sides(p):
            gated_copy(0, part, p).start()
            gated_copy(1, part, p).start()

        each_peer(both_sides)
        gated_copy(1, part, me).start()
    gated[0, me] = gated_send[pl.ds(me * per, per)]
    out.pass_weights(range(3))

    def take_gated(part):
        for side in (0, 1):
            each_peer(lambda p: gated_arrive(side, part, p).wait_recv())
            if side:
                gated_arrive(1, part, me).wait_recv()
            for q in range(part * few, (part + 1) * few):
                rows_first = gated[side, :, q].reshape(slab, RADIX).astype(F32)
                out.g2[side, q * RADIX : (q + 1) * RADIX, :] = rows_first.T.astype(BF)

    out.finish(take_gated)

    for g in range(3):
        each_peer(lambda p: project_copy(g, p).wait_send())
    for part in (0, 1):
        for side in (0, 1):
            each_peer(lambda p: gated_copy(side, part, p).wait_send())
        gated_copy(1, part, me).wait_send()


def operator_rows(
    n_seq, n_ch, tokens, in_weight, short_taps, band_freq, filter_first, filter_bias, filter_out, decay, out_weight
):
    rows, width = tokens.shape
    slab = in_weight.shape[2]
    channels = slab // n_seq
    per = rows // RADIX
    points = per * n_seq
    tables = dft_tables(points)
    anyspec = pl.BlockSpec(memory_space=pl.ANY)
    vspec = pl.BlockSpec(memory_space=pltpu.VMEM)
    dma = pltpu.SemaphoreType.DMA
    scratch = [
        pltpu.VMEM((rows, width), BF),
        pltpu.VMEM((3, width, slab), BF),
        pltpu.VMEM(short_taps.shape, F32),
        pltpu.VMEM((1, band_freq.shape[0]), F32),
        pltpu.VMEM(filter_first.shape, F32),
        pltpu.VMEM((1, filter_bias.shape[0]), F32),
        pltpu.VMEM(filter_out.shape, F32),
        pltpu.VMEM((1, slab), F32),
        *[pltpu.VMEM(t.shape, t.dtype) for t in tables],
        pltpu.VMEM((3, 3, slab, RADIX), F32),
        pltpu.VMEM((slab, filter_out.shape[0]), F32),
        pltpu.VMEM((slab, RADIX), F32),
        pltpu.VMEM((3, (points + 1) * channels, RADIX), F32),
        pltpu.VMEM((3, n_seq, per, channels, RADIX), BF),
        pltpu.VMEM((3, points, channels, RADIX), BF),
        pltpu.VMEM((points, channels, RADIX), BF),
        pltpu.VMEM((2, n_seq, per, channels, RADIX), BF),
        pltpu.VMEM((points * channels, RADIX), F32),
        pltpu.VMEM((points, channels * RADIX), BF),
        pltpu.VMEM((2 * HALF, channels * RADIX), F32),
        pltpu.VMEM((channels * HALF, 2 * RADIX), BF),
        pltpu.VMEM((channels * HALF, 2 * RADIX), F32),
        pltpu.VMEM((channels * HALF, 2 * RADIX), F32),
        dma((16,)), dma((3, n_seq)), dma((3, n_seq)), dma((2, 2, n_seq)), dma((2, 2, n_seq)),
        *spread_scratch(n_ch, rows, slab, out_weight.shape[1] // n_ch),
    ]
    return pl.pallas_call(
        functools.partial(operator_kernel, n_seq, n_ch),
        out_shape=pltpu.VMEM((rows, slab), BF),
        in_specs=[anyspec] * 14,
        out_specs=vspec,
        scratch_shapes=scratch,
        compiler_params=pltpu.CompilerParams(collective_id=0, has_side_effects=True, vmem_limit_bytes=56 * 2**20),
        cost_estimate=pl.CostEstimate(flops=2 * rows * width * slab * 3, bytes_accessed=12 * 2**20, transcendentals=0),
    )(
        tokens, jnp.transpose(in_weight, (1, 0, 2)), short_taps, band_freq[None, :], filter_first, filter_bias[None, :],
        filter_out, decay[None, :], *tables, out_weight,
    )


def local(tokens, in_weight, short_taps, band_freq, filter_first, filter_bias, filter_out, decay, out_weight):
    return operator_rows(
        lax.axis_size("seq"), lax.axis_size("ch"), tokens, in_weight, short_taps, band_freq, filter_first, filter_bias,
        filter_out, decay, out_weight,
    )


def solution(mesh):
    in_specs = (
        P("seq", None),
        P(None, None, "ch"),
        P(None, None, "ch"),
        P(),
        P(),
        P(),
        P(None, "ch"),
        P("ch"),
        P("ch", None),
    )
    out_specs = P("seq", "ch")
    return jax.shard_map(local, mesh=mesh, in_specs=in_specs, out_specs=out_specs, check_vma=False)
```

```python
import functools
import math

import jax
import jax.numpy as jnp
import numpy as np
from jax import lax
from jax.experimental import pallas as pl
from jax.experimental.pallas import tpu as pltpu
from jax.sharding import PartitionSpec as P

MESH = pl.DeviceIdType.MESH
BF = jnp.bfloat16
F32 = jnp.float32
HIGH = lax.Precision.HIGHEST
RADIX = 128
HALF = 80


def dft_tables(rows_in):
    full = RADIX * RADIX
    k1 = np.arange(HALF)[:, None]
    used = (k1 <= RADIX // 2).astype(np.float64)
    line = np.arange(RADIX)
    a = 2 * np.pi * k1 * np.arange(rows_in)[None, :] / RADIX
    outer = np.concatenate([np.cos(a) * used, -np.sin(a) * used], 0)
    tw = 2 * np.pi * k1 * line[None, :] / full
    twist = np.stack([np.cos(tw), np.sin(tw)])
    b = 2 * np.pi * np.outer(line, line) / RADIX
    co, si = np.cos(b), np.sin(b)
    inner = np.block([[co, -si], [si, co]])
    inner_back = np.block([[co, si], [-si, co]])
    weight = np.where((k1 == 0) | (k1 == RADIX // 2), 1.0, 2.0) * used / full
    outer_back = np.concatenate([(np.cos(a) * weight).T, (-np.sin(a) * weight).T], 1)
    return (
        jnp.asarray(outer, BF),
        jnp.asarray(twist, F32),
        jnp.asarray(inner, BF),
        jnp.asarray(inner_back, BF),
        jnp.asarray(outer_back, BF),
    )


def sin_turns(turns):
    turns = turns - 0.25
    turns = turns - jnp.round(turns)
    x = (0.25 - jnp.abs(turns)) * (2.0 * math.pi)
    x2 = x * x
    p = jnp.float32(-2.50521083854e-8)
    for c in (2.75573192239858e-6, -1.98412698412698e-4, 8.33333333333333e-3, -1.66666666666667e-1):
        p = p * x2 + jnp.float32(c)
    return x + x * x2 * p


def first_row(v):
    row = lax.broadcasted_iota(jnp.int32, (8, v.shape[1]), 0)
    return jnp.where(row == 0, jnp.broadcast_to(v, (8, v.shape[1])), 0.0)


def contract_rows(a, b):
    return lax.dot_general(a, b, (((0,), (0,)), ((), ())), precision=HIGH, preferred_element_type=F32)


def outer_product(v, w):
    return contract_rows(first_row(v), first_row(w))


def forward(grid32, x_all, a_all, rows_all, outer, twist, inner, spec_ref, channels):
    rows_in = x_all.shape[0]
    for c in range(channels):
        x_all[:, c * RADIX : (c + 1) * RADIX] = grid32[pl.ds(c, rows_in, stride=channels), :].astype(BF)
    a_all[...] = jnp.dot(outer[...], x_all[...], preferred_element_type=F32)
    co, si = twist[0], twist[1]
    for c in range(channels):
        lanes = slice(c * RADIX, (c + 1) * RADIX)
        re, im = a_all[:HALF, lanes], a_all[HALF:, lanes]
        rows = slice(c * HALF, (c + 1) * HALF)
        rows_all[rows, :RADIX] = (re * co + im * si).astype(BF)
        rows_all[rows, RADIX:] = (im * co - re * si).astype(BF)
    spec_ref[...] = jnp.dot(rows_all[...], inner[...], preferred_element_type=F32)


CHUNK = 256


class Spread:
    def __init__(self, n_ch, w_hbm, out_ref, wout, g2, sums, landed, wl_sem, wx_ssem, wx_rsem, wc_ssem, wc_rsem, r_ssem, r_rsem):
        self.__dict__.update(locals())
        del self.__dict__["self"]
        self.n_z = n_ch // 2
        self.c = lax.axis_index("ch")
        self.z = self.c // 2
        self.xl = lax.rem(self.c, 2)
        self.s = lax.axis_index("seq")
        self.core = lax.rem(self.s, 2)
        self.across = self.c + 1 - 2 * self.xl
        far = lax.rem(self.s // 2, 2)
        self.sides = [(self.s, self.across), (self.s + 2 - 4 * far, self.across)]
        self.sibling = {"seq": self.s + 1 - 2 * self.core}
        self.up = {"ch": lax.rem(self.c + 2, n_ch)}
        self.down = {"ch": lax.rem(self.c + n_ch - 2, n_ch)}
        self.depth = w_hbm.shape[0]
        self.cols = w_hbm.shape[1] // n_ch
        self.rows = out_ref.shape[0]
        self.chunks = self.rows // CHUNK
        half = self.n_z // 2
        shifts = [half] + [x for k in range(half - 1, 0, -1) for x in (k, self.n_z - k)] + [0]
        self.need = [lax.rem(self.z + k, self.n_z) for k in shifts]

    def _columns(self, block):
        return pl.ds(pl.multiple_of(block * self.cols, self.cols), self.cols)

    def own_weight(self, j):
        return pltpu.make_async_copy(
            self.w_hbm.at[:, self._columns(2 * j + self.xl)], self.wout.at[0, j], self.wl_sem.at[j]
        )

    def weight_to_side(self, k, side):
        j = self.need[k]
        part = self.depth // 4
        line = pl.ds(pl.multiple_of(self.core * 2 * part + side * part, part), part)
        return pltpu.make_async_remote_copy(
            src_ref=self.w_hbm.at[line, self._columns(2 * j + 1 - self.xl)],
            dst_ref=self.wout.at[1, j, line, :],
            send_sem=self.wx_ssem.at[side, k], recv_sem=self.wx_rsem.at[side, k],
            device_id=self.sides[side], device_id_type=MESH,
        )

    def weight_to_sibling(self, k, core):
        half = self.depth // 2
        piece = self.wout.at[1, self.need[k], pl.ds(pl.multiple_of(core * half, half), half), :]
        return pltpu.make_async_remote_copy(
            src_ref=piece, dst_ref=piece, send_sem=self.wc_ssem.at[k], recv_sem=self.wc_rsem.at[k],
            device_id=self.sibling, device_id_type=MESH,
        )

    def start_weights(self, blocks):
        for k in blocks:
            for side in (0, 1):
                self.weight_to_side(k, side).start()

    def load_weights(self):
        for j in range(self.n_z):
            self.own_weight(j).start()

    def pass_weights(self, blocks):
        for k in blocks:
            for side in (0, 1):
                self.weight_to_side(k, side).wait()
            self.weight_to_sibling(k, self.core).start()

    def take_weights(self, blocks):
        for k in blocks:
            self.weight_to_sibling(k, self.core).wait_send()
            self.weight_to_sibling(k, 1 - self.core).wait_recv()

    def hop(self, way, step, i):
        return pltpu.make_async_remote_copy(
            src_ref=self.sums.at[way, step, i], dst_ref=self.landed.at[way, step, i],
            send_sem=self.r_ssem.at[way, step, i], recv_sem=self.r_rsem.at[way, step, i],
            device_id=(self.up, self.down)[way], device_id_type=MESH,
        )

    def partial_sum(self, block, i):
        line = pl.ds(pl.multiple_of(i * CHUNK, CHUNK), CHUNK)
        return jnp.dot(self.g2[0, line], self.wout[0, block], preferred_element_type=F32) + jnp.dot(
            self.g2[1, line], self.wout[1, block], preferred_element_type=F32
        )

    def block_at(self, way, step):
        n = self.n_z
        if way == 0:
            return lax.rem(self.z + n // 2 - step, n)
        return lax.rem(self.z + n // 2 + step, n)

    def send(self, way, step, i, fresh):
        own = self.partial_sum(self.block_at(way, step), i)
        if not fresh:
            self.hop(way, step - 1, i).wait_recv()
            own = own + self.landed[way, step - 1, i].astype(F32)
        self.sums[way, step, i] = own.astype(BF)
        self.hop(way, step, i).start()

    def finish(self, take_gated):
        for j in range(self.n_z):
            self.own_weight(j).wait()
        half = self.chunks // 2

        def both(steps, firsts, fresh):
            def body(i, carry):
                for way in (0, 1):
                    self.send(way, steps[way], i if firsts[way] else half + i, fresh)
                return carry

            lax.fori_loop(0, half, body, 0)

        self.take_weights([0, 1, 2])
        take_gated(0)
        both((0, 1), (True, True), True)
        take_gated(1)
        both((1, 0), (False, False), True)
        self.pass_weights(range(3, self.n_z))
        both((1, 1), (True, False), False)
        steps = self.n_z // 2
        for step in range(2, steps):
            self.take_weights([2 * step - 1, 2 * step])
            both((step, step), (False, True), False)
            both((step, step), (True, False), False)
        self.take_weights([self.n_z - 1])

        def home(i, carry):
            own = self.partial_sum(self.z, i)
            self.hop(0, steps - 1, i).wait_recv()
            self.hop(1, steps - 1, i).wait_recv()
            own = own + self.landed[0, steps - 1, i].astype(F32) + self.landed[1, steps - 1, i].astype(F32)
            self.out_ref[pl.ds(pl.multiple_of(i * CHUNK, CHUNK), CHUNK), :] = own.astype(BF)
            return carry

        lax.fori_loop(0, self.chunks, home, 0)

        def drain(i, carry):
            for step in range(1, steps):
                self.hop(0, step, i).wait_send()
                self.hop(1, step, i).wait_send()
            return carry

        lax.fori_loop(0, self.chunks, drain, 0)

        def drain_first(i, carry):
            self.hop(0, 0, i).wait_send()
            self.hop(1, 0, half + i).wait_send()
            return carry

        lax.fori_loop(0, half, drain_first, 0)


def spread_scratch(n_ch, rows, depth, cols):
    n_z = n_ch // 2
    dma = pltpu.SemaphoreType.DMA
    return [
        pltpu.VMEM((2, n_z, depth, cols), BF),
        pltpu.VMEM((2, rows, depth), BF),
        pltpu.VMEM((2, n_z // 2, rows // CHUNK, CHUNK, cols), BF),
        pltpu.VMEM((2, n_z // 2, rows // CHUNK, CHUNK, cols), BF),
        dma((n_z,)), dma((2, n_z)), dma((2, n_z)), dma((n_z,)), dma((n_z,)),
        dma((2, n_z // 2, rows // CHUNK)), dma((2, n_z // 2, rows // CHUNK)),
    ]


def operator_kernel(
    n_seq, n_ch,
    tok_hbm, w_hbm, taps_hbm, band_hbm, first_hbm, bias_hbm, fout_hbm, decay_hbm, outer_hbm, twist_hbm, inner_hbm, inner_back_hbm, outer_back_hbm, wout_hbm,
    out_ref,
    tok, w, taps, band, first, bias, fout, decay, outer, twist, inner, inner_back, outer_back,
    tap_cols, fout_rows, decay_cols, padded, send4, pro_recv, gated_send, gated,
    grid32, x_all, a_all, rows_all, imp_spec, src_spec,
    load_sem, pro_ssem, pro_rsem, gat_ssem, gat_rsem, *out_scratch,
):
    me = lax.axis_index("seq")
    out = Spread(n_ch, wout_hbm, out_ref, *out_scratch)
    rows, width = tok_hbm.shape
    slab = w_hbm.shape[2]
    channels = slab // n_seq
    per = rows // RADIX
    points = per * n_seq
    half = rows // 2
    length = rows * n_seq

    loads = [
        pltpu.make_async_copy(w_hbm.at[0], w.at[0], load_sem.at[0]),
        pltpu.make_async_copy(tok_hbm.at[:half], tok.at[:half], load_sem.at[1]),
        pltpu.make_async_copy(tok_hbm.at[half:], tok.at[half:], load_sem.at[2]),
        pltpu.make_async_copy(w_hbm.at[2], w.at[2], load_sem.at[3]),
        pltpu.make_async_copy(w_hbm.at[1], w.at[1], load_sem.at[4]),
        pltpu.make_async_copy(outer_hbm, outer, load_sem.at[5]),
        pltpu.make_async_copy(twist_hbm, twist, load_sem.at[6]),
        pltpu.make_async_copy(inner_hbm, inner, load_sem.at[7]),
        pltpu.make_async_copy(inner_back_hbm, inner_back, load_sem.at[8]),
        pltpu.make_async_copy(outer_back_hbm, outer_back, load_sem.at[9]),
    ]
    small = [
        pltpu.make_async_copy(a, b, load_sem.at[10 + i])
        for i, (a, b) in enumerate(
            [(taps_hbm, taps), (fout_hbm, fout), (decay_hbm, decay), (band_hbm, band), (first_hbm, first), (bias_hbm, bias)]
        )
    ]
    for copy in loads[:2] + small + loads[2:]:
        copy.start()

    barrier = pltpu.get_barrier_semaphore()

    def greet(d, carry):
        pl.semaphore_signal(barrier, inc=1, device_id={"seq": lax.rem(me + d, n_seq)}, device_id_type=MESH)
        return carry

    lax.fori_loop(1, n_seq, greet, 0)

    def greet_across(p, carry):
        pl.semaphore_signal(barrier, inc=1, device_id=(p, out.across), device_id_type=MESH)
        return carry

    lax.fori_loop(0, n_seq, greet_across, 0)
    for peer in (out.up, out.down):
        pl.semaphore_signal(barrier, inc=1, device_id=peer, device_id_type=MESH)

    for copy in small:
        copy.wait()
    for g in range(3):
        for i in range(3):
            tap_cols[g, i] = jnp.broadcast_to(taps[i, g : g + 1, :], (RADIX, slab)).T
        padded[g, 0:channels, :] = jnp.zeros((channels, RADIX), F32)
    fout_rows[...] = fout[...].T
    decay_cols[...] = jnp.broadcast_to(decay[...], (RADIX, slab)).T

    mine = pl.ds(pl.multiple_of(me * channels, channels), channels)

    def spread_copy(src, dst, ssem, rsem, peer):
        return pltpu.make_async_remote_copy(
            src_ref=src.at[peer],
            dst_ref=dst.at[pl.ds(me * per, per)],
            send_sem=ssem.at[peer],
            recv_sem=rsem.at[me],
            device_id={"seq": peer},
            device_id_type=MESH,
        )

    def arrive(dst, ssem, rsem, peer):
        piece = dst.at[pl.ds(peer * per, per)]
        return pltpu.make_async_remote_copy(
            src_ref=piece, dst_ref=piece, send_sem=ssem.at[peer], recv_sem=rsem.at[peer],
            device_id={"seq": peer}, device_id_type=MESH,
        )

    def own_piece(src, dst):
        dst[pl.ds(me * per, per)] = src[me]

    def each_peer(step):
        def body(d, carry):
            step(lax.rem(me + d, n_seq))
            return carry

        lax.fori_loop(1, n_seq, body, 0)

    def project(g):
        for part in (0, 1):
            if g == 0:
                loads[1 + part].wait()
            y = jnp.dot(tok[part * half : (part + 1) * half, :], w[g], preferred_element_type=F32)
            for q in range(per // 2):
                piece = y[q * RADIX : (q + 1) * RADIX, :].T.astype(BF)
                send4[g, :, part * (per // 2) + q] = piece.reshape(n_seq, channels, RADIX)

    def project_copy(g, p):
        return spread_copy(send4.at[g], pro_recv.at[g], pro_ssem.at[g], pro_rsem.at[g], p)

    def mixed(g, row, count):
        lane = lax.broadcasted_iota(jnp.int32, (count, RADIX), 1)
        now = padded[g, pl.ds(channels + row, count), :]
        before = padded[g, pl.ds(row, count), :]
        total = jnp.zeros((count // channels, channels, RADIX), F32)
        for i in range(3):
            moved = now if i == 0 else pltpu.roll(jnp.where(lane >= RADIX - i, before, now), i, 1)
            total = total + tap_cols[g, i, mine, :][None] * moved.reshape(count // channels, channels, RADIX)
        return total.reshape(count, RADIX)

    def take_projected(g):
        each_peer(lambda p: arrive(pro_recv.at[g], pro_ssem.at[g], pro_rsem.at[g], p).wait_recv())
        padded[g, channels:, :] = pro_recv[g].astype(F32).reshape(points * channels, RADIX)

    block = 8 * channels

    def each_block(step):
        def body(i, carry):
            step(pl.multiple_of(i * block, block))
            return carry

        lax.fori_loop(0, points * channels // block, body, 0)

    n_band = band.shape[1]
    stretch = 2 * rows

    def filter_block(step, carry):
        pos = (step * stretch + lax.broadcasted_iota(jnp.int32, (1, stretch), 1)).astype(F32)
        scaled = pos * (1.0 / length)
        turns = outer_product(band[...], scaled)
        turns = turns - jnp.round(turns)
        head = lax.broadcasted_iota(jnp.int32, (8, stretch), 0)
        features = jnp.concatenate(
            [sin_turns(turns + 0.25), sin_turns(turns), jnp.where(head == 0, scaled, jnp.where(head == 1, 1.0, 0.0))], 0
        )
        head = lax.broadcasted_iota(jnp.int32, (8, first.shape[1]), 0)
        layer = jnp.concatenate(
            [
                first[1 : 1 + n_band, :],
                first[1 + n_band :, :],
                jnp.where(head == 0, first[0:1, :], jnp.where(head == 1, bias[...], 0.0)),
            ],
            0,
        )
        hidden = sin_turns(contract_rows(layer, features) * (1.0 / (2.0 * math.pi)))
        shaped = jnp.dot(fout_rows[mine, :], hidden, precision=HIGH, preferred_element_type=F32)
        fall = -decay_cols[mine, :]
        for q in range(stretch // RADIX):
            lanes = slice(q * RADIX, (q + 1) * RADIX)
            row = pl.multiple_of((step * (stretch // RADIX) + q) * channels, channels)
            grid32[pl.ds(row, channels), :] = shaped[:, lanes] * jnp.exp(fall * pos[:, lanes])
        return carry

    loads[0].wait()
    project(0)
    pl.semaphore_wait(barrier, 2 * n_seq + 1)
    each_peer(lambda p: project_copy(0, p).start())
    loads[3].wait()
    project(2)
    each_peer(lambda p: project_copy(2, p).start())
    out.start_weights(range(3))
    loads[4].wait()
    project(1)
    each_peer(lambda p: project_copy(1, p).start())
    out.start_weights(range(3, out.n_z))
    out.load_weights()
    for g in range(3):
        own_piece(send4.at[g], pro_recv.at[g])
    for copy in loads[5:]:
        copy.wait()

    lax.fori_loop(0, length // stretch, filter_block, 0)
    forward(grid32, x_all, a_all, rows_all, outer, twist, inner, imp_spec, channels)

    take_projected(0)
    take_projected(2)

    def source_block(row):
        grid32[pl.ds(row, block), :] = mixed(0, row, block) * mixed(2, row, block)

    each_block(source_block)
    forward(grid32, x_all, a_all, rows_all, outer, twist, inner, src_spec, channels)

    for c in range(channels):
        line = slice(c * HALF, (c + 1) * HALF)
        sre, sim = src_spec[line, :RADIX], src_spec[line, RADIX:]
        ire, iim = imp_spec[line, :RADIX], imp_spec[line, RADIX:]
        rows_all[line, :RADIX] = (sre * ire - sim * iim).astype(BF)
        rows_all[line, RADIX:] = (sre * iim + sim * ire).astype(BF)
    src_spec[...] = jnp.dot(rows_all[...], inner_back[...], preferred_element_type=F32)
    co, si = twist[0], twist[1]
    for c in range(channels):
        line = slice(c * HALF, (c + 1) * HALF)
        lanes = slice(c * RADIX, (c + 1) * RADIX)
        re, im = src_spec[line, :RADIX], src_spec[line, RADIX:]
        back = jnp.concatenate([re * co - im * si, im * co + re * si], 0).astype(BF)
        y = jnp.dot(outer_back[...], back, preferred_element_type=F32)
        grid32[pl.ds(c, points, stride=channels), :] = y
    take_projected(1)

    def gate_block(row):
        value = grid32[pl.ds(row, block), :] * mixed(1, row, block)
        gated_send[pl.ds(row // channels, 8)] = value.astype(BF).reshape(8, channels, RADIX)

    each_block(gate_block)

    few = per // 2

    def gated_copy(side, part, peer):
        return pltpu.make_async_remote_copy(
            src_ref=gated_send.at[pl.ds(peer * per + part * few, few)],
            dst_ref=gated.at[side, me, part * few : (part + 1) * few],
            send_sem=gat_ssem.at[side, part, peer],
            recv_sem=gat_rsem.at[side, part, me],
            device_id=(peer, out.across if side else out.c),
            device_id_type=MESH,
        )

    def gated_arrive(side, part, peer):
        piece = gated.at[side, peer, part * few : (part + 1) * few]
        return pltpu.make_async_remote_copy(
            src_ref=piece, dst_ref=piece, send_sem=gat_ssem.at[side, part, peer], recv_sem=gat_rsem.at[side, part, peer],
            device_id=(peer, out.across if side else out.c), device_id_type=MESH,
        )

    for part in (0, 1):

        def both_sides(p):
            gated_copy(1, part, p).start()
            gated_copy(0, part, p).start()

        each_peer(both_sides)
        gated_copy(1, part, me).start()
    gated[0, me] = gated_send[pl.ds(me * per, per)]
    out.pass_weights(range(3))

    def take_gated(part):
        for side in (1, 0):
            each_peer(lambda p: gated_arrive(side, part, p).wait_recv())
            if side:
                gated_arrive(1, part, me).wait_recv()
            for q in range(part * few, (part + 1) * few):
                rows_first = gated[side, :, q].reshape(slab, RADIX).astype(F32)
                out.g2[side, q * RADIX : (q + 1) * RADIX, :] = rows_first.T.astype(BF)

    out.finish(take_gated)

    for g in range(3):
        each_peer(lambda p: project_copy(g, p).wait_send())
    for part in (0, 1):
        for side in (0, 1):
            each_peer(lambda p: gated_copy(side, part, p).wait_send())
        gated_copy(1, part, me).wait_send()


def operator_rows(
    n_seq, n_ch, tokens, in_weight, short_taps, band_freq, filter_first, filter_bias, filter_out, decay, out_weight
):
    rows, width = tokens.shape
    slab = in_weight.shape[2]
    channels = slab // n_seq
    per = rows // RADIX
    points = per * n_seq
    tables = dft_tables(points)
    anyspec = pl.BlockSpec(memory_space=pl.ANY)
    vspec = pl.BlockSpec(memory_space=pltpu.VMEM)
    dma = pltpu.SemaphoreType.DMA
    scratch = [
        pltpu.VMEM((rows, width), BF),
        pltpu.VMEM((3, width, slab), BF),
        pltpu.VMEM(short_taps.shape, F32),
        pltpu.VMEM((1, band_freq.shape[0]), F32),
        pltpu.VMEM(filter_first.shape, F32),
        pltpu.VMEM((1, filter_bias.shape[0]), F32),
        pltpu.VMEM(filter_out.shape, F32),
        pltpu.VMEM((1, slab), F32),
        *[pltpu.VMEM(t.shape, t.dtype) for t in tables],
        pltpu.VMEM((3, 3, slab, RADIX), F32),
        pltpu.VMEM((slab, filter_out.shape[0]), F32),
        pltpu.VMEM((slab, RADIX), F32),
        pltpu.VMEM((3, (points + 1) * channels, RADIX), F32),
        pltpu.VMEM((3, n_seq, per, channels, RADIX), BF),
        pltpu.VMEM((3, points, channels, RADIX), BF),
        pltpu.VMEM((points, channels, RADIX), BF),
        pltpu.VMEM((2, n_seq, per, channels, RADIX), BF),
        pltpu.VMEM((points * channels, RADIX), F32),
        pltpu.VMEM((points, channels * RADIX), BF),
        pltpu.VMEM((2 * HALF, channels * RADIX), F32),
        pltpu.VMEM((channels * HALF, 2 * RADIX), BF),
        pltpu.VMEM((channels * HALF, 2 * RADIX), F32),
        pltpu.VMEM((channels * HALF, 2 * RADIX), F32),
        dma((16,)), dma((3, n_seq)), dma((3, n_seq)), dma((2, 2, n_seq)), dma((2, 2, n_seq)),
        *spread_scratch(n_ch, rows, slab, out_weight.shape[1] // n_ch),
    ]
    return pl.pallas_call(
        functools.partial(operator_kernel, n_seq, n_ch),
        out_shape=pltpu.VMEM((rows, slab), BF),
        in_specs=[anyspec] * 14,
        out_specs=vspec,
        scratch_shapes=scratch,
        compiler_params=pltpu.CompilerParams(collective_id=0, has_side_effects=True, vmem_limit_bytes=56 * 2**20),
        cost_estimate=pl.CostEstimate(flops=2 * rows * width * slab * 3, bytes_accessed=12 * 2**20, transcendentals=0),
    )(
        tokens, jnp.transpose(in_weight, (1, 0, 2)), short_taps, band_freq[None, :], filter_first, filter_bias[None, :],
        filter_out, decay[None, :], *tables, out_weight,
    )


def local(tokens, in_weight, short_taps, band_freq, filter_first, filter_bias, filter_out, decay, out_weight):
    return operator_rows(
        lax.axis_size("seq"), lax.axis_size("ch"), tokens, in_weight, short_taps, band_freq, filter_first, filter_bias,
        filter_out, decay, out_weight,
    )


def solution(mesh):
    in_specs = (
        P("seq", None),
        P(None, None, "ch"),
        P(None, None, "ch"),
        P(),
        P(),
        P(),
        P(None, "ch"),
        P("ch"),
        P("ch", None),
    )
    out_specs = P("seq", "ch")
    return jax.shard_map(local, mesh=mesh, in_specs=in_specs, out_specs=out_specs, check_vma=False)
```
